128 devices in a mesh: src: 8 (over z_lo, x), snk: 16 (over y, z_hi, core).
Axes of the slice: x: 4, y: 4, z: 4 (z_hi: 2, z_lo: 2; z = z_hi * 2 + z_lo), core: 2. Of those that a mesh axis runs over, the one named last changes fastest.
Arguments:
- perambulator: bfloat16 [8, 16, 2, 1024, 1024], P('src', 'snk'), may hold values from -0.25976562 to 0.25976562
- elementals: bfloat16 [16, 4, 2, 256, 256], P('snk', None, None, 'src'), may hold values from -0.25 to 0.25
- momentum: int32 [16], P('snk'), may hold values from 0 to 3
- routes: int32 [8, 16, 16, 1], P('src'), may hold values from 0 to 15; in each aligned block of 16 rows (0 to 15, 16 to 31, ..., all dimensions but the last counted through in order) at most 2 rows name the same one
- node_of: int32 [8, 16, 16], P('src'), may hold values from 0 to 15
- owner_slot: int32 [16], replicated, may hold values from 0 to 15, each once
Outputs:
- nodes: float32 [16, 2, 64, 1024], P('snk', None, 'src')
The draws below stay inside these ranges and needn't reach their ends.
Inputs may be any that keep to these rules, and one draw needn't show every extreme that they name: `routes`: among the 16 slabs of one tile (one s and k), at most 2 name the same sink timeslice. `owner_slot`: each value appears exactly once.
All inputs are finite; a program needn't handle non-finite values.
Results may differ from the reference program's by a relative error of at most 0.005.
Values may be sent and summed in bfloat16 or wider, within the bound.
A program may use at most 128 MiB of HBM per device.

```python
import math
import jax
import jax.numpy as jnp
import numpy as np
from jax import lax

NEV = 256
SPIN = 4
M = 1024
NMOM = 4
RB = 64
NB = 16
CAP = 2
NNODE = 16
NS = 8
NK = 16


def place_ends(drawn, stream_key, least, largest):
    place = [jax.random.randint(jax.random.fold_in(stream_key, axis), (), 0, length) for axis, length in enumerate(drawn.shape)]
    main_axis = drawn.shape.index(max(drawn.shape))
    neighbour = place[:main_axis] + [(place[main_axis] + 1) % drawn.shape[main_axis]] + place[main_axis + 1:]
    return drawn.at[tuple(place)].set(least).at[tuple(neighbour)].set(largest)


def block_scale(rng, dims, pieces, low, largest):
    def one(dim, blocks):
        draws = jax.random.uniform(jax.random.fold_in(jax.random.fold_in(rng, 6), dim), (blocks,), jnp.float32, low / len(pieces), largest / len(pieces))
        return jnp.repeat(jnp.exp(draws), dims[dim] // blocks).reshape((-1,) + (1,) * (len(dims) - dim - 1))

    gain = one(*pieces[0])
    for cut in pieces[1:]:
        gain = gain * one(*cut)
    return gain


def deal_out(key, own, number, rows, count, top, bound, slope):
    ranking = jax.random.permutation(key, count)
    heavy_load, common = load_shares(count, rows * top, bound, slope, True), load_shares(count, rows * top, bound, slope, False)
    places = jnp.arange(count)

    def named(tallies, rotation):
        used = int((tallies > 0).sum())
        fixed = max(1, used // 4)
        moved = fixed + (places - fixed + rotation * (used - fixed)) % max(1, count - fixed)
        return jnp.zeros((count,), jnp.int32).at[ranking[jnp.where(places < fixed, places, moved)]].set(jnp.asarray(tallies, jnp.int32))

    tallies = jnp.where(number % 4 == 0, named(heavy_load, number // 4), named(common, number - number // 4 - 1))
    mixed = jax.random.permutation(jax.random.fold_in(own, 3), count)
    giver, receiver = mixed[0:count // 2 * 2:2], mixed[1:count // 2 * 2:2]
    margin = jnp.minimum(tallies[giver] - 1, bound - tallies[receiver]) // 2
    margin = jnp.where((giver == ranking[0]) | (receiver == ranking[0]) | (tallies[receiver] == 0), 0, jnp.maximum(margin, 0))
    moved = jax.random.randint(jax.random.fold_in(own, 4), (count // 2,), 0, 1 << 20) % (margin + 1)
    tallies = tallies.at[giver].add(-moved).at[receiver].add(moved)
    labels = jnp.searchsorted(jnp.cumsum(tallies), jnp.arange(rows * top), side="right").astype(jnp.int32)
    table = labels.reshape(top, rows).T
    table = table[jax.random.permutation(jax.random.fold_in(own, 1), rows)]
    rotation = jax.random.randint(jax.random.fold_in(own, 2), (rows, 1), 0, top)
    return jnp.take_along_axis(table, (jnp.arange(top)[None, :] + rotation) % top, axis=1)


def load_shares(number_of, total, bound, skew, full):
    portions = [(1 << 20) // math.isqrt(grade ** skew) + 1 for grade in range(1, number_of + 1)]
    largest = bound if full else min(bound, max(-(-total // number_of), total * portions[0] // sum(portions)))
    least = 1 if total - largest >= number_of - 1 else 0
    given, rest = [largest] + [least] * (number_of - 1), total - largest - least * (number_of - 1)
    while rest > 0:
        movable = [i for i in range(1, number_of) if given[i] < largest] or [i for i in range(1, number_of) if given[i] < bound]
        pool, left = sum([portions[i] for i in movable]), rest
        for i in movable:
            more = min(bound - given[i], max(1, left * portions[i] // pool), rest)
            given[i] = given[i] + more
            rest = rest - more
    return np.array(given)


def normal_values(stream_key, dims, spread, reach, pieces=(), held_as=jnp.bfloat16):
    array = jax.random.normal(stream_key, dims, jnp.float32) * spread
    if len(pieces) > 0:
        array = block_scale(stream_key, dims, pieces, -0.22, 0.18) * array
    return jnp.clip(array, min=-reach, max=reach).astype(held_as)


def setup_inputs(seed: int = 0) -> dict:
    key_of = jax.random.split(jax.random.key(seed), 7)
    perambulator = normal_values(key_of[0], (NS, NK, 2, M, M), 0.044, 0.25976562, ((0, 8), (1, 16)))
    elementals = normal_values(key_of[1], (NK, NMOM, 2, NEV, NEV), (2 * NEV) ** -0.5, 0.25, ((0, 16), (3, 8)))
    momentum = place_ends(jax.random.randint(key_of[2], (NK,), 0, NMOM), jax.random.fold_in(key_of[2], 1), 0, NMOM - 1).astype(jnp.int32)
    routes_keys = jax.random.split(jax.random.fold_in(key_of[3], 1), NS * NK * NB // NB)
    routes_turns = jax.random.permutation(jax.random.fold_in(key_of[3], 3), NS * NK * NB // NB)
    routes = jax.vmap(lambda own, number: deal_out(jax.random.fold_in(key_of[3], 2), own, number, NB, NK, 1, CAP, 2))(routes_keys, routes_turns).reshape((NS, NK, NB, 1))
    node_of = place_ends(jax.random.randint(key_of[4], (NS, NK, NB), 0, NNODE), jax.random.fold_in(key_of[4], 1), 0, NNODE - 1).astype(jnp.int32)
    owner_slot = jax.random.permutation(key_of[5], NNODE).astype(jnp.int32)
    return dict(perambulator=perambulator, elementals=elementals, momentum=momentum, routes=routes, node_of=node_of, owner_slot=owner_slot)


def dress(phi, source_tile):
    right = source_tile.reshape(2, NEV, SPIN * M)
    real_part = jnp.dot(phi[0], right[0], preferred_element_type=jnp.float32) - jnp.dot(phi[1], right[1], preferred_element_type=jnp.float32)
    imag_part = jnp.dot(phi[0], right[1], preferred_element_type=jnp.float32) + jnp.dot(phi[1], right[0], preferred_element_type=jnp.float32)
    return jnp.stack([real_part, imag_part]).astype(jnp.bfloat16).reshape(2, M, M)


def times_adjoint(slab_rows, partner):
    real_part = jnp.dot(slab_rows[0], partner[0].T, preferred_element_type=jnp.float32) + jnp.dot(slab_rows[1], partner[1].T, preferred_element_type=jnp.float32)
    imag_part = jnp.dot(slab_rows[1], partner[0].T, preferred_element_type=jnp.float32) - jnp.dot(slab_rows[0], partner[1].T, preferred_element_type=jnp.float32)
    return jnp.stack([real_part, imag_part])


def reference(perambulator, elementals, momentum, routes, node_of, owner_slot):
    sinks = jnp.arange(NK, dtype=jnp.int32)
    phis = elementals[sinks, momentum.astype(jnp.int32)]

    def per_source(source, totals):
        tiles = perambulator[source]
        dressed = lax.map(lambda pair: dress(pair[0], pair[1]), (phis, tiles))
        slabs = dressed.reshape(NK, 2, NB, RB, M)

        def per_slab(index, inner):
            sink = (index // NB).astype(jnp.int32)
            block = (index % NB).astype(jnp.int32)
            chosen = slabs[sink][:, block]
            helper = routes[source, sink, block, 0].astype(jnp.int32)
            partner = dressed[helper]
            product = times_adjoint(chosen, partner)
            position = owner_slot[node_of[source, sink, block]].astype(jnp.int32)
            return inner.at[position].add(product)

        return lax.fori_loop(0, NK * NB, per_slab, totals)

    start = jnp.zeros((NNODE, 2, RB, M), jnp.float32)
    return lax.fori_loop(0, NS, per_source, start)
```

```python
import jax
import jax.numpy as jnp
from jax import lax
from jax.experimental import pallas as pl
from jax.experimental.pallas import tpu as pltpu
from jax.sharding import PartitionSpec as P

MESH = pl.DeviceIdType.MESH
F32 = jnp.float32
BF16 = jnp.bfloat16
PIECES = 4


def iota(shape, dim):
    return lax.broadcasted_iota(jnp.int32, shape, dim)


def dot(a, b):
    return jnp.dot(a, b, preferred_element_type=F32)


def dot_nt(a, b):
    return lax.dot_general(a, b, (((1,), (1,)), ((), ())), preferred_element_type=F32)


def kernel(
    momentum, owner_slot, elementals, routes, node_of, tile_hbm, out_ref,
    tile, phi, spread, kron, place, select, order, lane_order,
    sent, held, gathered, factor, kept, core_out, core_in,
    x_out, x_in, own_sum, y_out, y_in, z_out, z_in,
    tile_sem, phi_s, phi_r, ex_s, ex_r, core_s, core_r, x_s, x_r, y_s, y_r, z_s, z_r,
):
    source = lax.axis_index("src")
    sink = lax.axis_index("snk")
    zl, xx = source // 4, source % 4
    yy, zh, core = sink // 4, (sink // 2) % 2, sink % 2

    load = pltpu.make_async_copy(tile_hbm, tile, tile_sem)
    load.start()

    barrier = pltpu.get_barrier_semaphore()

    def greet_source(n, _):
        pl.semaphore_signal(barrier, inc=1, device_id=((source + n) % 8, sink), device_id_type=MESH)
        return 0

    def greet_sink(n, _):
        pl.semaphore_signal(barrier, inc=1, device_id=(source, (sink + n) % 16), device_id_type=MESH)
        return 0

    def at_z(zlo, zhi):
        return (zlo * 4 + xx, (yy * 2 + zhi) * 2 + core)

    lax.fori_loop(1, 8, greet_source, 0)
    lax.fori_loop(1, 16, greet_sink, 0)
    pl.semaphore_signal(barrier, inc=1, device_id=at_z(1 - zl, 1 - zh), device_id_type=MESH)

    phi[source] = elementals[momentum[0]]
    pl.semaphore_wait(barrier, 23)

    def phi_copy(n, owner):
        return pltpu.make_async_remote_copy(
            src_ref=phi.at[owner], dst_ref=phi.at[owner],
            send_sem=phi_s.at[n], recv_sem=phi_r.at[n],
            device_id=((source + n) % 8, sink), device_id_type=MESH,
        )

    def phi_start(n, _):
        phi_copy(n, source).start()
        return 0

    lax.fori_loop(1, 8, phi_start, 0)

    spread[...] = jnp.where(iota((256, 1024), 1) // 4 == iota((256, 1024), 0), 1.0, 0.0).astype(BF16)
    position = jnp.zeros((16, 16), jnp.int32)
    for node in range(16):
        position = position + jnp.where(node_of[...] == node, owner_slot[node], 0)
    code = routes[...] * 16 + (position % 2) * 8 + position // 2
    widen = jnp.where(iota((16, 256), 1) % 16 == iota((16, 256), 0), 1.0, 0.0).astype(BF16)
    wide = dot(code.astype(F32).astype(BF16), widen)
    wide = jnp.where(iota((16, 256), 1) // 16 == iota((16, 256), 0), wide, 0.0)
    named = jnp.sum(wide, axis=0, keepdims=True).astype(jnp.int32)
    select[...] = jnp.where(iota((256, 256), 0) == named, 1.0, 0.0).astype(BF16)
    row = iota((256, 256), 0)
    order[...] = jnp.where(iota((256, 256), 1) == (row % 16) * 16 + row // 16, 1.0, 0.0).astype(BF16)

    def phi_wait(n, _):
        copy = phi_copy(n, (source + 8 - n) % 8)
        copy.wait_recv()
        return 0

    lax.fori_loop(1, 8, phi_wait, 0)
    load.wait()

    low_lanes = iota((256, 128), 1) < 64

    def ex_copy(n, dest, origin):
        return pltpu.make_async_remote_copy(
            src_ref=sent.at[n, dest], dst_ref=held.at[n, origin],
            send_sem=ex_s.at[n, dest], recv_sem=ex_r.at[n, origin],
            device_id=(source, dest), device_id_type=MESH,
        )

    def dress(n, _):
        t = (xx + 1 + n) % 4
        rows = iota((256, 256), 0)
        il, b = rows // 16, rows % 16
        e = b * 16 + (il // 8) * 8 + t * 2 + (il % 8) // 4
        place[...] = jnp.where(iota((256, 256), 1) == e, 1.0, 0.0).astype(BF16)
        spins = iota((256, 1024), 1) % 4 == (iota((256, 1024), 0) // 16) % 4
        for part in range(2):
            whole = jnp.concatenate([phi[q, part] for q in range(8)], axis=0)
            placed = dot(place[...], whole).astype(BF16)
            grown = dot(placed, spread[...])
            kron[part * 256:(part + 1) * 256, :] = jnp.where(spins, grown, 0.0).astype(BF16)

        def columns(chip):
            lanes = pl.ds(pl.multiple_of(chip * 128, 128), 128)
            right = jnp.concatenate([tile[0, :, lanes], tile[1, :, lanes]], axis=1)
            both = dot(kron[...], right)
            real = both[:256, :128] - both[256:, 128:]
            imag = both[:256, 128:] + both[256:, :128]
            low = jnp.where(low_lanes, real, pltpu.roll(imag, 64, 1)).astype(BF16)
            high = jnp.where(low_lanes, pltpu.roll(real, 64, 1), imag).astype(BF16)
            return low, high

        def remote(h, _):
            chip = ((yy + h // 2 + 1) % 4) * 2 + (zh + h + 1) % 2
            low, high = columns(chip)
            sent[n, 2 * chip] = low
            sent[n, 2 * chip + 1] = high
            ex_copy(n, 2 * chip, sink).start()
            ex_copy(n, 2 * chip + 1, sink).start()
            return 0

        lax.fori_loop(0, 7, remote, 0)
        chip = yy * 2 + zh
        low, high = columns(chip)
        held[n, sink] = jnp.where(core == 0, low, high)
        sent[n, sink + 1 - 2 * core] = jnp.where(core == 0, high, low)
        ex_copy(n, sink + 1 - 2 * core, sink).start()
        return 0

    lax.fori_loop(0, PIECES, dress, 0)

    for t in range(4):
        r = iota((256, 1024), 0)
        target = (r % 16) * 64 + (r // 128) * 32 + t * 8 + (r // 16) % 8
        lane_order[t] = jnp.where(iota((256, 1024), 1) == target, 1.0, 0.0).astype(BF16)

    def core_copy(g):
        return pltpu.make_async_remote_copy(
            src_ref=core_out.at[g], dst_ref=core_in.at[g],
            send_sem=core_s.at[g], recv_sem=core_r.at[g],
            device_id=(source, sink + 1 - 2 * core), device_id_type=MESH,
        )

    def x_copy(ni, tj):
        return pltpu.make_async_remote_copy(
            src_ref=x_out.at[ni, tj], dst_ref=x_in.at[ni, tj],
            send_sem=x_s.at[ni, tj], recv_sem=x_r.at[ni, tj],
            device_id=(zl * 4 + (xx + 1 + ni) % 4, sink), device_id_type=MESH,
        )

    def settle(g, ni, nj):
        core_copy(g).wait_recv()
        total = kept[g] + core_in[g].astype(F32)
        tj = (xx + 1 + nj) % 4

        @pl.when(ni < 3)
        def _():
            x_out[ni, tj] = total.astype(BF16)
            x_copy(ni, tj).start()

        @pl.when(ni == 3)
        def _():
            own_sum[tj] = total

    def pair(n, g):
        ni = jnp.where(g <= n, n, g - n - 1)
        nj = jnp.where(g <= n, g, n)
        return ni, nj

    def piece(n, _):
        def arrive(o, _):
            origin = (sink + o) % 16
            ex_copy(n, sink, origin).wait_recv()
            return 0

        lax.fori_loop(1, 16, arrive, 0)

        def collect(pairing, _):
            first = pl.ds(pl.multiple_of(pairing * 32, 32), 16)
            second = pl.ds(pl.multiple_of(pairing * 32 + 16, 16), 16)
            left = held[n, :, first, :].reshape(256, 128)
            right = held[n, :, second, :].reshape(256, 128)
            sums = dot(select[...], jnp.concatenate([left, right], axis=1)).astype(BF16)
            for r in range(16):
                lanes = slice(r * 128, (r + 1) * 128)
                gathered[first, lanes] = sums[r * 16:(r + 1) * 16, :128]
                gathered[second, lanes] = sums[r * 16:(r + 1) * 16, 128:]
            return 0

        lax.fori_loop(0, 8, collect, 0)

        def arrange(r, _):
            lanes = pl.ds(pl.multiple_of(r * 128, 128), 128)
            plain = dot(order[...], gathered[:, lanes])
            turned = pltpu.roll(plain, 64, 1)
            turned = jnp.where(low_lanes, turned, -turned)
            both = jnp.stack([plain.reshape(32, 8, 128), turned.reshape(32, 8, 128)], axis=1)
            factor[n, :, lanes] = both.reshape(512, 128).astype(BF16)
            return 0

        lax.fori_loop(0, 16, arrange, 0)

        def block(g, _):
            ni, nj = pair(n, g)
            number = n * n + g
            right = jnp.concatenate([held[nj, r] for r in range(16)], axis=1)
            product = dot_nt(factor[ni], right)
            kept[number] = jnp.where(core == 0, product[:256], product[256:])
            core_out[number] = jnp.where(core == 0, product[256:], product[:256]).astype(BF16)
            core_copy(number).start()

            @pl.when(g > 0)
            def _():
                pi, pj = pair(n, g - 1)
                settle(number - 1, pi, pj)

            return 0

        lax.fori_loop(0, 2 * n + 1, block, 0)
        li, lj = pair(n, 2 * n)
        settle(n * n + 2 * n, li, lj)
        return 0

    lax.fori_loop(0, PIECES, piece, 0)

    def x_arrive(tj, total):
        summed = own_sum[tj]
        for ni in range(3):
            x_copy(ni, tj).wait_recv()
            summed = summed + x_in[ni, tj].astype(F32)
        return total + dot(summed.astype(BF16), lane_order[tj])

    whole = lax.fori_loop(0, 4, x_arrive, jnp.zeros((256, 1024), F32))
    y_out[...] = whole.reshape(4, 64, 1024).astype(BF16)

    def y_copy(n):
        return pltpu.make_async_remote_copy(
            src_ref=y_out.at[(yy + n) % 4], dst_ref=y_in.at[n - 1],
            send_sem=y_s.at[n - 1], recv_sem=y_r.at[n - 1],
            device_id=(source, ((yy + n) % 4) * 4 + zh * 2 + core), device_id_type=MESH,
        )

    for n in range(1, 4):
        y_copy(n).start()
    summed = y_out[yy].astype(F32)
    for n in range(1, 4):
        y_copy(n).wait_recv()
        summed = summed + y_in[n - 1].astype(F32)
    z_out[...] = summed.reshape(4, 16, 1024)

    def z_copy(n):
        z = zh * 2 + zl
        there = (z + n) % 4
        return pltpu.make_async_remote_copy(
            src_ref=z_out.at[there], dst_ref=z_in.at[n - 1],
            send_sem=z_s.at[n - 1], recv_sem=z_r.at[n - 1],
            device_id=at_z(there % 2, there // 2), device_id_type=MESH,
        )

    for n in range(1, 4):
        z_copy(n).start()
    final = z_out[zh * 2 + zl]
    for n in range(1, 4):
        z_copy(n).wait_recv()
        final = final + z_in[n - 1]
    out_ref[...] = final.reshape(2, 8, 1024)

    def phi_done(n, _):
        phi_copy(n, source).wait_send()
        return 0

    lax.fori_loop(1, 8, phi_done, 0)

    def ex_done(n, _):
        def one(o, _):
            ex_copy(n, (sink + o) % 16, sink).wait_send()
            return 0

        lax.fori_loop(1, 16, one, 0)
        return 0

    lax.fori_loop(0, PIECES, ex_done, 0)

    def core_done(g, _):
        core_copy(g).wait_send()
        return 0

    lax.fori_loop(0, 16, core_done, 0)

    def x_done(g, _):
        x_copy(g // 4, g % 4).wait_send()
        return 0

    lax.fori_loop(0, 12, x_done, 0)
    for n in range(1, 4):
        y_copy(n).wait_send()
        z_copy(n).wait_send()


def on_device(perambulator, elementals, momentum, routes, node_of, owner_slot):
    vmem = pl.BlockSpec(memory_space=pltpu.VMEM)
    smem = pl.BlockSpec(memory_space=pltpu.SMEM)
    dma = pltpu.SemaphoreType.DMA
    out = pl.pallas_call(
        kernel,
        out_shape=jax.ShapeDtypeStruct((2, 8, 1024), F32),
        in_specs=[smem, smem, vmem, vmem, vmem, pl.BlockSpec(memory_space=pl.ANY)],
        out_specs=vmem,
        scratch_shapes=[
            pltpu.VMEM((2, 1024, 1024), BF16),
            pltpu.VMEM((8, 2, 32, 256), BF16),
            pltpu.VMEM((256, 1024), BF16),
            pltpu.VMEM((512, 1024), BF16),
            pltpu.VMEM((256, 256), BF16),
            pltpu.VMEM((256, 256), BF16),
            pltpu.VMEM((256, 256), BF16),
            pltpu.VMEM((4, 256, 1024), BF16),
            pltpu.VMEM((4, 16, 256, 128), BF16),
            pltpu.VMEM((4, 16, 256, 128), BF16),
            pltpu.VMEM((256, 2048), BF16),
            pltpu.VMEM((4, 512, 2048), BF16),
            pltpu.VMEM((16, 256, 256), F32),
            pltpu.VMEM((16, 256, 256), BF16),
            pltpu.VMEM((16, 256, 256), BF16),
            pltpu.VMEM((3, 4, 256, 256), BF16),
            pltpu.VMEM((3, 4, 256, 256), BF16),
            pltpu.VMEM((4, 256, 256), F32),
            pltpu.VMEM((4, 64, 1024), BF16),
            pltpu.VMEM((3, 64, 1024), BF16),
            pltpu.VMEM((4, 16, 1024), F32),
            pltpu.VMEM((3, 16, 1024), F32),
            dma, dma((8,)), dma((8,)), dma((4, 16)), dma((4, 16)),
            dma((16,)), dma((16,)), dma((3, 4)), dma((3, 4)),
            dma((3,)), dma((3,)), dma((3,)), dma((3,)),
        ],
        compiler_params=pltpu.CompilerParams(
            collective_id=0, has_side_effects=True, vmem_limit_bytes=60 * 2**20
        ),
        cost_estimate=pl.CostEstimate(flops=20 * 10**9, bytes_accessed=8 * 2**20, transcendentals=0),
    )(
        momentum,
        owner_slot,
        elementals[0],
        routes[0, :, :, 0],
        node_of[0],
        perambulator[0, 0],
    )
    return out[None]


def solution(mesh):
    placed = (
        P("src", "snk", None, None, None),
        P("snk", None, None, "src", None),
        P("snk"),
        P("src", None, None, None),
        P("src", None, None),
        P(),
    )
    return jax.shard_map(
        on_device,
        mesh=mesh,
        in_specs=placed,
        out_specs=P("snk", None, "src", None),
        check_vma=False,
    )
```

```python
import jax
import jax.numpy as jnp
from jax import lax
from jax.experimental import pallas as pl
from jax.experimental.pallas import tpu as pltpu
from jax.sharding import PartitionSpec as P

MESH = pl.DeviceIdType.MESH
F32 = jnp.float32
BF16 = jnp.bfloat16
PIECES = 4
STEPS_Y = sum(dy << (2 * h) for h, dy in enumerate((2, 1, 1, 3, 3, 2, 0)))


def iota(shape, dim):
    return lax.broadcasted_iota(jnp.int32, shape, dim)


def dot(a, b):
    return jnp.dot(a, b, preferred_element_type=F32)


def dot_nt(a, b):
    return lax.dot_general(a, b, (((1,), (1,)), ((), ())), preferred_element_type=F32)


def kernel(
    momentum, owner_slot, elementals, routes, node_of, tile_hbm, out_ref,
    tile, right, phi, placed, select, rows_order, lane_order,
    sent, held, factor, kept, core_out, core_in,
    x_out, x_in, own_sum, last_out, last_in,
    tile_sem, phi_s, phi_r, ex_s, ex_r, core_s, core_r, x_s, x_r, last_s, last_r,
):
    source = lax.axis_index("src")
    sink = lax.axis_index("snk")
    zl, xx = source // 4, source % 4
    yy, zh, core = sink // 4, (sink // 2) % 2, sink % 2

    load = pltpu.make_async_copy(tile_hbm, tile, tile_sem)
    load.start()

    barrier = pltpu.get_barrier_semaphore()

    def greet(there):
        pl.semaphore_signal(barrier, inc=1, device_id=there, device_id_type=MESH)

    def greet_source(n, _):
        greet(((source + n) % 8, sink))
        return 0

    def greet_sink(n, _):
        greet((source, (sink + n) % 16))
        return 0

    def greet_other(n, _):
        greet(((source + 4) % 8, (sink + 2 * n) % 16))
        return 0

    lax.fori_loop(1, 8, greet_source, 0)
    lax.fori_loop(1, 16, greet_sink, 0)
    lax.fori_loop(1, 8, greet_other, 0)

    phi[source] = elementals[momentum[0]]
    pl.semaphore_wait(barrier, 29)

    def phi_copy(n, owner):
        return pltpu.make_async_remote_copy(
            src_ref=phi.at[owner], dst_ref=phi.at[owner],
            send_sem=phi_s.at[n], recv_sem=phi_r.at[n],
            device_id=((source + n) % 8, sink), device_id_type=MESH,
        )

    def phi_start(n, _):
        phi_copy(n, source).start()
        return 0

    lax.fori_loop(1, 8, phi_start, 0)

    row, col = iota((256, 256), 0), iota((256, 256), 1)

    spins = jnp.where(col == (row & 63) * 4 + (row >> 6), 1.0, 0.0).astype(BF16)
    load.wait()

    def by_spin(chip, _):
        lanes = pl.ds(pl.multiple_of(chip * 128, 128), 128)
        for part in range(4):
            rows = slice(part * 256, (part + 1) * 256)
            both = jnp.concatenate([tile[0, rows, lanes], tile[1, rows, lanes]], axis=1)
            sorted_rows = dot(spins, both).astype(BF16)
            for a in range(4):
                right[chip, a, part * 64:(part + 1) * 64] = sorted_rows[a * 64:(a + 1) * 64]
        return 0

    lax.fori_loop(0, 8, by_spin, 0)

    t = (xx + 1 + (row >> 6)) & 3
    wanted = (row & 15) * 16 + ((row >> 5) & 1) * 8 + t * 2 + ((row >> 4) & 1)
    place = jnp.where(col == wanted, 1.0, 0.0).astype(BF16)

    def phi_wait(n, _):
        phi_copy(n, (source + 8 - n) % 8).wait_recv()
        return 0

    lax.fori_loop(1, 8, phi_wait, 0)
    for part in range(2):
        whole = jnp.concatenate([phi[q, part] for q in range(8)], axis=0)
        placed[part * 256:(part + 1) * 256, :] = dot(place, whole).astype(BF16)

    low_lanes = iota((256, 128), 1) < 64

    def ex_copy(n, dest, origin):
        return pltpu.make_async_remote_copy(
            src_ref=sent.at[n, dest], dst_ref=held.at[n, origin],
            send_sem=ex_s.at[n, dest], recv_sem=ex_r.at[n, origin],
            device_id=(source, dest), device_id_type=MESH,
        )

    def chip_at(h):
        dy = (STEPS_Y >> (2 * h)) & 3
        return ((yy + dy) % 4) * 2 + (zh + h + 1) % 2

    def columns(chip, a):
        both = dot(placed[...], right[chip, a])
        real = both[:256, :128] - both[256:, 128:]
        imag = both[:256, 128:] + both[256:, :128]
        low = jnp.where(low_lanes, real, pltpu.roll(imag, 64, 1)).astype(BF16)
        high = jnp.where(low_lanes, pltpu.roll(real, 64, 1), imag).astype(BF16)
        return low, high

    def dress(h, _):
        chip = chip_at(h)
        for a in range(4):
            low, high = columns(chip, a)
            for n in range(PIECES):
                sent[n, 2 * chip, a * 64:(a + 1) * 64] = low[n * 64:(n + 1) * 64]
                sent[n, 2 * chip + 1, a * 64:(a + 1) * 64] = high[n * 64:(n + 1) * 64]
        ex_copy(0, 2 * chip, sink).start()
        ex_copy(0, 2 * chip + 1, sink).start()
        return 0

    lax.fori_loop(0, 7, dress, 0)
    partner = sink + 1 - 2 * core
    for a in range(4):
        low, high = columns(yy * 2 + zh, a)
        mine = jnp.where(core == 0, low, high)
        theirs = jnp.where(core == 0, high, low)
        for n in range(PIECES):
            held[n, sink, a * 64:(a + 1) * 64] = mine[n * 64:(n + 1) * 64]
            sent[n, partner, a * 64:(a + 1) * 64] = theirs[n * 64:(n + 1) * 64]
    ex_copy(0, partner, sink).start()

    def send(n, _):
        def one(h, _):
            ex_copy(n, 2 * chip_at(h % 7) + h // 7, sink).start()
            return 0

        lax.fori_loop(0, 14, one, 0)
        ex_copy(n, partner, sink).start()
        return 0

    lax.fori_loop(1, PIECES, send, 0)

    position = jnp.zeros((16, 16), jnp.int32)
    for node in range(16):
        position = position + jnp.where(node_of[...] == node, owner_slot[node], 0)
    code = routes[...] * 16 + (position & 1) * 8 + (position >> 1)
    slab_row, slab_lane = iota((16, 256), 0), iota((16, 256), 1)
    widen = jnp.where((slab_lane & 15) == slab_row, 1.0, 0.0).astype(BF16)
    wide = dot(code.astype(F32).astype(BF16), widen)
    wide = jnp.where((slab_lane >> 4) == slab_row, wide, 0.0)
    named = jnp.sum(wide, axis=0, keepdims=True).astype(jnp.int32)
    select[...] = jnp.where(row == named, 1.0, 0.0).astype(BF16)

    spin, z_low, half, part, y_zh = row & 3, (row >> 4) & 1, (row >> 2) & 1, (row >> 3) & 1, row >> 5
    came = (spin << 6) | (z_low << 5) | (half << 4) | (part << 3) | y_zh
    rows_order[...] = jnp.where(col == came, 1.0, 0.0).astype(BF16)
    r, lane = iota((256, 1024), 0), iota((256, 1024), 1)
    target = (r & 15) * 64 + ((r >> 5) & 1) * 32 + ((r >> 4) & 1) * 4 + (r >> 6)
    for t in range(4):
        lane_order[t * 256:(t + 1) * 256] = jnp.where(lane == target + t * 8, 1.0, 0.0).astype(BF16)

    def core_copy(g):
        return pltpu.make_async_remote_copy(
            src_ref=core_out.at[g], dst_ref=core_in.at[g],
            send_sem=core_s.at[g], recv_sem=core_r.at[g],
            device_id=(source, partner), device_id_type=MESH,
        )

    def x_copy(ni, tj):
        return pltpu.make_async_remote_copy(
            src_ref=x_out.at[ni, tj], dst_ref=x_in.at[ni, tj],
            send_sem=x_s.at[ni, tj], recv_sem=x_r.at[ni, tj],
            device_id=(zl * 4 + (xx + 1 + ni) % 4, sink), device_id_type=MESH,
        )

    def settle(g, ni, nj):
        core_copy(g).wait_recv()
        total = kept[g] + core_in[g].astype(F32)
        tj = (xx + 1 + nj) % 4

        @pl.when(ni < 3)
        def _():
            x_out[ni, tj] = total.astype(BF16)
            x_copy(ni, tj).start()

        @pl.when(ni == 3)
        def _():
            own_sum[tj] = total

    def block(number, ni, nj):
        side = jnp.concatenate([held[nj, r] for r in range(16)], axis=1)
        product = dot_nt(factor[ni], side)
        kept[number] = jnp.where(core == 0, product[:256], product[256:])
        core_out[number] = jnp.where(core == 0, product[256:], product[:256]).astype(BF16)
        core_copy(number).start()

    def piece(n, _):
        def arrive(o, _):
            ex_copy(n, sink, (sink + o) % 16).wait_recv()
            return 0

        lax.fori_loop(1, 16, arrive, 0)

        def earlier(m, _):
            number = n * n + m
            block(number, m, n)
            pi = jnp.where(m == 0, n - 1, m - 1)
            pj = jnp.where(m == 0, n - 1, n)
            settle(number - 1, pi, pj)
            return 0

        lax.fori_loop(0, n, earlier, 0)

        def collect(pairing, _):
            first = pl.ds(pl.multiple_of(pairing * 32, 32), 16)
            second = pl.ds(pl.multiple_of(pairing * 32 + 16, 16), 16)
            pair = [held[n, :, first, :].reshape(256, 128), held[n, :, second, :].reshape(256, 128)]
            sums = dot(select[...], jnp.concatenate(pair, axis=1))
            for k in range(2):
                plain = sums[:, k * 128:(k + 1) * 128]
                turned = pltpu.roll(plain, 64, 1)
                turned = jnp.where(low_lanes, turned, -turned)
                both = jnp.stack([plain.reshape(32, 8, 128), turned.reshape(32, 8, 128)], axis=1).astype(BF16)
                for r in range(16):
                    for c in range(2):
                        rows = pl.ds(pl.multiple_of(c * 256 + pairing * 32 + k * 16, 16), 16)
                        factor[n, rows, r * 128:(r + 1) * 128] = both[2 * r + c].reshape(16, 128)
            return 0

        lax.fori_loop(0, 8, collect, 0)

        def later(m, _):
            number = n * n + n + m
            block(number, n, m)

            @pl.when(number > 0)
            def _():
                pi = jnp.where(m == 0, n - 1, n)
                pj = jnp.where(m == 0, n, m - 1)
                settle(number - 1, pi, pj)

            return 0

        lax.fori_loop(0, n + 1, later, 0)
        return 0

    lax.fori_loop(0, PIECES, piece, 0)
    settle(15, 3, 3)

    arrived = []
    for tj in range(4):
        summed = own_sum[tj]
        for ni in range(3):
            x_copy(ni, tj).wait_recv()
            summed = summed + x_in[ni, tj].astype(F32)
        arrived.append(dot(rows_order[...], summed.astype(BF16)).astype(BF16))
    whole = dot(jnp.concatenate(arrived, axis=1), lane_order[...])
    last_out[...] = whole.reshape(16, 16, 1024).astype(BF16)

    mine = yy * 4 + zh * 2 + zl

    def last_copy(n):
        there = (mine + n) % 16
        return pltpu.make_async_remote_copy(
            src_ref=last_out.at[there], dst_ref=last_in.at[n],
            send_sem=last_s.at[n], recv_sem=last_r.at[n],
            device_id=((there % 2) * 4 + xx, (there // 2) * 2 + core), device_id_type=MESH,
        )

    def last_start(n, _):
        last_copy(n).start()
        return 0

    lax.fori_loop(1, 16, last_start, 0)

    def last_sum(n, total):
        last_copy(n).wait_recv()
        return total + last_in[n].astype(F32)

    final = lax.fori_loop(1, 16, last_sum, last_out[mine].astype(F32))
    out_ref[...] = final.reshape(2, 8, 1024)

    def phi_done(n, _):
        phi_copy(n, source).wait_send()
        return 0

    lax.fori_loop(1, 8, phi_done, 0)

    def ex_done(n, _):
        def one(o, _):
            ex_copy(n, (sink + o) % 16, sink).wait_send()
            return 0

        lax.fori_loop(1, 16, one, 0)
        return 0

    lax.fori_loop(0, PIECES, ex_done, 0)

    def core_done(g, _):
        core_copy(g).wait_send()
        return 0

    lax.fori_loop(0, 16, core_done, 0)

    def x_done(g, _):
        x_copy(g // 4, g % 4).wait_send()
        return 0

    lax.fori_loop(0, 12, x_done, 0)

    def last_done(n, _):
        last_copy(n).wait_send()
        return 0

    lax.fori_loop(1, 16, last_done, 0)


def on_device(perambulator, elementals, momentum, routes, node_of, owner_slot):
    vmem = pl.BlockSpec(memory_space=pltpu.VMEM)
    smem = pl.BlockSpec(memory_space=pltpu.SMEM)
    dma = pltpu.SemaphoreType.DMA
    out = pl.pallas_call(
        kernel,
        out_shape=jax.ShapeDtypeStruct((2, 8, 1024), F32),
        in_specs=[smem, smem, vmem, vmem, vmem, pl.BlockSpec(memory_space=pl.ANY)],
        out_specs=vmem,
        scratch_shapes=[
            pltpu.VMEM((2, 1024, 1024), BF16),
            pltpu.VMEM((8, 4, 256, 256), BF16),
            pltpu.VMEM((8, 2, 32, 256), BF16),
            pltpu.VMEM((512, 256), BF16),
            pltpu.VMEM((256, 256), BF16),
            pltpu.VMEM((256, 256), BF16),
            pltpu.VMEM((1024, 1024), BF16),
            pltpu.VMEM((4, 16, 256, 128), BF16),
            pltpu.VMEM((4, 16, 256, 128), BF16),
            pltpu.VMEM((4, 512, 2048), BF16),
            pltpu.VMEM((16, 256, 256), F32),
            pltpu.VMEM((16, 256, 256), BF16),
            pltpu.VMEM((16, 256, 256), BF16),
            pltpu.VMEM((3, 4, 256, 256), BF16),
            pltpu.VMEM((3, 4, 256, 256), BF16),
            pltpu.VMEM((4, 256, 256), F32),
            pltpu.VMEM((16, 16, 1024), BF16),
            pltpu.VMEM((16, 16, 1024), BF16),
            dma, dma((8,)), dma((8,)), dma((4, 16)), dma((4, 16)),
            dma((16,)), dma((16,)), dma((3, 4)), dma((3, 4)),
            dma((16,)), dma((16,)),
        ],
        compiler_params=pltpu.CompilerParams(
            collective_id=0, has_side_effects=True, vmem_limit_bytes=60 * 2**20
        ),
        cost_estimate=pl.CostEstimate(flops=20 * 10**9, bytes_accessed=8 * 2**20, transcendentals=0),
    )(
        momentum,
        owner_slot,
        elementals[0],
        routes[0, :, :, 0],
        node_of[0],
        perambulator[0, 0],
    )
    return out[None]


def solution(mesh):
    placed = (
        P("src", "snk", None, None, None),
        P("snk", None, None, "src", None),
        P("snk"),
        P("src", None, None, None),
        P("src", None, None),
        P(),
    )
    return jax.shard_map(
        on_device,
        mesh=mesh,
        in_specs=placed,
        out_specs=P("snk", None, "src", None),
        check_vma=False,
    )
```

```python
import jax
import jax.numpy as jnp
from jax import lax
from jax.experimental import pallas as pl
from jax.experimental.pallas import tpu as pltpu
from jax.sharding import PartitionSpec as P

MESH = pl.DeviceIdType.MESH
F32 = jnp.float32
BF16 = jnp.bfloat16
PIECES = 4
WINDOW = 24


def packed(values, bits):
    return sum(value << (bits * n) for n, value in enumerate(values))


CHIPS = ((0, 1), (1, 1), (1, 0), (2, 1), (3, 1), (2, 0), (3, 0))
CHIPS_Y = packed([c[0] for c in CHIPS], 2)
CHIPS_Z = packed([c[1] for c in CHIPS], 1)
PEERS = (
    (0, 1, 0), (1, 1, 0), (1, 0, 0), (2, 1, 0), (3, 1, 0), (2, 0, 0), (0, 1, 1), (1, 1, 1),
    (3, 0, 0), (2, 1, 1), (3, 1, 1), (1, 0, 1), (2, 0, 1), (3, 0, 1), (0, 0, 1),
)
PEERS_Y = packed([p[0] for p in PEERS], 2)
PEERS_Z = packed([p[1] for p in PEERS], 1)
PEERS_C = packed([p[2] for p in PEERS], 1)

def iota(shape, dim):
    return lax.broadcasted_iota(jnp.int32, shape, dim)


def dot(a, b):
    return jnp.dot(a, b, preferred_element_type=F32)


def dot_nt(a, b):
    return lax.dot_general(a, b, (((1,), (1,)), ((), ())), preferred_element_type=F32)


def kernel(
    momentum, owner_slot, elementals, routes, node_of, tile_hbm, out_ref,
    tile, right, phi, placed, select, rows_order, lane_order,
    sent, held, factor, kept, core_out, core_in,
    x_out, x_in, own_sum, last_out, last_in,
    tile_sem, phi_s, phi_r, ex_s, ex_r, core_s, core_r, x_s, x_r, last_s, last_r,
):
    source = lax.axis_index("src")
    sink = lax.axis_index("snk")
    zl, xx = source // 4, source % 4
    yy, zh, core = sink // 4, (sink // 2) % 2, sink % 2

    load = pltpu.make_async_copy(tile_hbm, tile, tile_sem)
    load.start()

    barrier = pltpu.get_barrier_semaphore()

    def greet(there):
        pl.semaphore_signal(barrier, inc=1, device_id=there, device_id_type=MESH)

    def greet_source(n, _):
        greet(((source + n) % 8, sink))
        return 0

    def greet_sink(n, _):
        greet((source, (sink + n) % 16))
        return 0

    def greet_other(n, _):
        greet(((source + 4) % 8, (sink + 2 * n) % 16))
        return 0

    lax.fori_loop(1, 8, greet_source, 0)
    lax.fori_loop(1, 16, greet_sink, 0)
    lax.fori_loop(1, 8, greet_other, 0)

    row, col = iota((256, 256), 0), iota((256, 256), 1)
    phi[source] = elementals[momentum[0]]

    def chip_at(h):
        dy, dz = (CHIPS_Y >> (2 * h)) & 3, (CHIPS_Z >> h) & 1
        return ((yy + dy) % 4) * 2 + (zh + dz) % 2

    def peer_at(j):
        dy, dz, dc = (PEERS_Y >> (2 * j)) & 3, (PEERS_Z >> j) & 1, (PEERS_C >> j) & 1
        return ((yy + dy) % 4) * 4 + ((zh + dz) % 2) * 2 + (core + dc) % 2

    spins = jnp.where(col == (row & 63) * 4 + (row >> 6), 1.0, 0.0).astype(BF16)

    def by_spin(h, _):
        chip = chip_at(h)
        lanes = pl.ds(pl.multiple_of(chip * 128, 128), 128)
        for part in range(4):
            rows = slice(part * 256, (part + 1) * 256)
            both = jnp.concatenate([tile[0, rows, lanes], tile[1, rows, lanes]], axis=1)
            sorted_rows = dot(spins, both).astype(BF16)
            for a in range(4):
                right[chip, a, part * 64:(part + 1) * 64] = sorted_rows[a * 64:(a + 1) * 64]
        return 0


    pl.semaphore_wait(barrier, 29)

    def phi_copy(n, owner):
        return pltpu.make_async_remote_copy(
            src_ref=phi.at[owner], dst_ref=phi.at[owner],
            send_sem=phi_s.at[n], recv_sem=phi_r.at[n],
            device_id=((source + n) % 8, sink), device_id_type=MESH,
        )

    def phi_start(n, _):
        phi_copy(n, source).start()
        return 0

    lax.fori_loop(1, 8, phi_start, 0)
    load.wait()
    lax.fori_loop(0, 8, by_spin, 0)

    t = (xx + 1 + (row >> 6)) & 3
    wanted = (row & 15) * 16 + ((row >> 5) & 1) * 8 + t * 2 + ((row >> 4) & 1)
    place = jnp.where(col == wanted, 1.0, 0.0).astype(BF16)

    def phi_wait(n, _):
        phi_copy(n, (source + 8 - n) % 8).wait_recv()
        return 0

    lax.fori_loop(1, 8, phi_wait, 0)
    for part in range(2):
        whole = jnp.concatenate([phi[q, part] for q in range(8)], axis=0)
        placed[part * 256:(part + 1) * 256, :] = dot(place, whole).astype(BF16)

    low_lanes = iota((256, 128), 1) < 64

    def ex_copy(n, dest, origin):
        return pltpu.make_async_remote_copy(
            src_ref=sent.at[n, dest], dst_ref=held.at[n, origin],
            send_sem=ex_s.at[n, dest], recv_sem=ex_r.at[n, origin],
            device_id=(source, dest), device_id_type=MESH,
        )

    def columns(chip, a):
        both = dot(placed[...], right[chip, a])
        real = both[:256, :128] - both[256:, 128:]
        imag = both[:256, 128:] + both[256:, :128]
        low = jnp.where(low_lanes, real, pltpu.roll(imag, 64, 1)).astype(BF16)
        high = jnp.where(low_lanes, pltpu.roll(real, 64, 1), imag).astype(BF16)
        return low, high

    def dress(h, _):
        chip = chip_at(h)
        for a in range(4):
            low, high = columns(chip, a)
            for n in range(PIECES):
                sent[n, 2 * chip, a * 64:(a + 1) * 64] = low[n * 64:(n + 1) * 64]
                sent[n, 2 * chip + 1, a * 64:(a + 1) * 64] = high[n * 64:(n + 1) * 64]
        ex_copy(0, 2 * chip, sink).start()
        ex_copy(0, 2 * chip + 1, sink).start()
        return 0

    lax.fori_loop(0, 7, dress, 0)
    partner = sink + 1 - 2 * core
    for a in range(4):
        low, high = columns(yy * 2 + zh, a)
        mine = jnp.where(core == 0, low, high)
        theirs = jnp.where(core == 0, high, low)
        for n in range(PIECES):
            held[n, sink, a * 64:(a + 1) * 64] = mine[n * 64:(n + 1) * 64]
            sent[n, partner, a * 64:(a + 1) * 64] = theirs[n * 64:(n + 1) * 64]
    ex_copy(0, partner, sink).start()

    def ex_send(q):
        return ex_copy(q // 15, peer_at(q % 15), sink)

    def ex_start(q, _):
        ex_send(q).start()
        return 0

    lax.fori_loop(15, WINDOW, ex_start, 0)

    position = jnp.zeros((16, 16), jnp.int32)
    for node in range(16):
        position = position + jnp.where(node_of[...] == node, owner_slot[node], 0)
    code = routes[...] * 16 + (position & 1) * 8 + (position >> 1)
    slab_row, slab_lane = iota((16, 256), 0), iota((16, 256), 1)
    widen = jnp.where((slab_lane & 15) == slab_row, 1.0, 0.0).astype(BF16)
    wide = dot(code.astype(F32).astype(BF16), widen)
    wide = jnp.where((slab_lane >> 4) == slab_row, wide, 0.0)
    named = jnp.sum(wide, axis=0, keepdims=True).astype(jnp.int32)
    select[...] = jnp.where(row == named, 1.0, 0.0).astype(BF16)

    spin, z_low, half, part, y_zh = row & 3, (row >> 4) & 1, (row >> 2) & 1, (row >> 3) & 1, row >> 5
    came = (spin << 6) | (z_low << 5) | (half << 4) | (part << 3) | y_zh
    rows_order[...] = jnp.where(col == came, 1.0, 0.0).astype(BF16)
    r, lane = iota((256, 1024), 0), iota((256, 1024), 1)
    target = (r & 15) * 64 + ((r >> 5) & 1) * 32 + ((r >> 4) & 1) * 4 + (r >> 6)
    for m in range(4):
        t = (xx + 4 - m) % 4
        lane_order[m * 256:(m + 1) * 256] = jnp.where(lane == target + t * 8, 1.0, 0.0).astype(BF16)

    def core_copy(g):
        return pltpu.make_async_remote_copy(
            src_ref=core_out.at[g], dst_ref=core_in.at[g],
            send_sem=core_s.at[g], recv_sem=core_r.at[g],
            device_id=(source, partner), device_id_type=MESH,
        )

    def x_copy(ni, tj):
        return pltpu.make_async_remote_copy(
            src_ref=x_out.at[ni, tj], dst_ref=x_in.at[ni, tj],
            send_sem=x_s.at[ni, tj], recv_sem=x_r.at[ni, tj],
            device_id=(zl * 4 + (xx + 1 + ni) % 4, sink), device_id_type=MESH,
        )

    def settle(g, ni, nj):
        core_copy(g).wait_recv()
        total = kept[g] + core_in[g].astype(F32)
        tj = (xx + 1 + nj) % 4

        @pl.when(ni < 3)
        def _():
            x_out[ni, tj] = total.astype(BF16)
            x_copy(ni, tj).start()

        @pl.when(ni == 3)
        def _():
            own_sum[tj] = total

    def block(number, ni, nj):
        side = jnp.concatenate([held[nj, r] for r in range(16)], axis=1)
        product = dot_nt(factor[ni], side)
        kept[number] = product[:256]
        core_out[number] = product[256:].astype(BF16)
        core_copy(number).start()

    def arrive(n):
        def one(o, _):
            ex_copy(n, sink, (sink + o) % 16).wait_recv()
            q = n * 15 + o - 1 + WINDOW

            @pl.when(q < 15 * PIECES)
            def _():
                ex_send(q - WINDOW).wait_send()
                ex_send(q).start()

            return 0

        lax.fori_loop(1, 16, one, 0)

    def earlier_blocks(n, base):
        def earlier(m, _):
            block(base + m, m, n)

            @pl.when(m > 0)
            def _():
                settle(base + m - 1, m - 1, n)

            return 0

        lax.fori_loop(0, n, earlier, 0)

    def collect_piece(n, halfway=None):
        def collect(pairing, _):
            first = pl.ds(pl.multiple_of(pairing * 32, 32), 16)
            second = pl.ds(pl.multiple_of(pairing * 32 + 16, 16), 16)
            pair = [held[n, :, first, :].reshape(256, 128), held[n, :, second, :].reshape(256, 128)]
            sums = dot(select[...], jnp.concatenate(pair, axis=1))
            for k in range(2):
                plain = sums[:, k * 128:(k + 1) * 128]
                turned = pltpu.roll(plain, 64, 1)
                turned = jnp.where(low_lanes, turned, -turned)
                both = jnp.stack([plain.reshape(32, 8, 128), turned.reshape(32, 8, 128)], axis=1).astype(BF16)
                for r in range(16):
                    for c in range(2):
                        rows = pl.ds(pl.multiple_of(((core + c) % 2) * 256 + pairing * 32 + k * 16, 16), 16)
                        factor[n, rows, r * 128:(r + 1) * 128] = both[2 * r + c].reshape(16, 128)
            return 0

        lax.fori_loop(0, 4, collect, 0)
        if halfway:
            halfway()
        lax.fori_loop(4, 8, collect, 0)

    def later_blocks(n, base, start, stop):
        def later(m, _):
            block(base + m, n, n - m)

            @pl.when(m > 0)
            def _():
                settle(base + m - 1, n, n - m + 1)

            return 0

        lax.fori_loop(start, stop, later, 0)

    def last_copy(side, n):
        there = (mine + n) % 16
        return pltpu.make_async_remote_copy(
            src_ref=last_out.at[side, there], dst_ref=last_in.at[side, n],
            send_sem=last_s.at[side, n], recv_sem=last_r.at[side, n],
            device_id=((there % 2) * 4 + xx, (there // 2) * 2 + core), device_id_type=MESH,
        )

    def sum_x(side):
        for k in range(2):
            tj = (xx + 4 - 2 * side - k) % 4
            summed = own_sum[tj]
            for ni in range(3):
                x_copy(ni, tj).wait_recv()
                summed = summed + x_in[ni, tj].astype(F32)
            ordered = dot(rows_order[...], summed.astype(BF16)).astype(BF16)
            last_out[side, :, :, k * 256:(k + 1) * 256] = ordered.reshape(16, 16, 256)

        def last_start(n, _):
            last_copy(side, n).start()
            return 0

        lax.fori_loop(1, 16, last_start, 0)

    def sum_yz(side):
        def last_sum(n, total):
            last_copy(side, n).wait_recv()
            return total + last_in[side, n].astype(F32)

        total = lax.fori_loop(1, 16, last_sum, last_out[side, mine].astype(F32))
        high = total.astype(BF16)
        rest = total - high.astype(F32)
        middle = rest.astype(BF16)
        low = (rest - middle.astype(F32)).astype(BF16)
        parts = dot(jnp.concatenate([high, middle, low], axis=0), lane_order[side * 512:(side + 1) * 512])
        return (parts[:16] + parts[16:32]) + parts[32:]

    mine = yy * 4 + zh * 2 + zl

    def piece(n, _):
        arrive(n)
        collect_piece(n)
        later_blocks(n, n * n, 0, n + 1)
        earlier_blocks(n, n * n + n + 1)
        settle(n * n + n, n, 0)

        @pl.when(n > 0)
        def _():
            settle(n * n + 2 * n, n - 1, n)

        return 0

    lax.fori_loop(0, 3, piece, 0)
    arrive(3)
    earlier_blocks(3, 9)
    collect_piece(3, lambda: settle(11, 2, 3))
    later_blocks(3, 12, 0, 3)
    sum_x(0)
    later_blocks(3, 12, 3, 4)
    settle(15, 3, 0)
    sum_x(1)
    final = sum_yz(0) + sum_yz(1)
    out_ref[...] = final.reshape(2, 8, 1024)

    def phi_done(n, _):
        phi_copy(n, source).wait_send()
        return 0

    lax.fori_loop(1, 8, phi_done, 0)

    def ex_done(q, _):
        ex_send(q).wait_send()
        return 0

    lax.fori_loop(15 * PIECES - WINDOW, 15 * PIECES, ex_done, 0)

    def core_done(g, _):
        core_copy(g).wait_send()
        return 0

    lax.fori_loop(0, 16, core_done, 0)

    def x_done(g, _):
        x_copy(g // 4, g % 4).wait_send()
        return 0

    lax.fori_loop(0, 12, x_done, 0)

    def last_done(n, _):
        last_copy(0, n).wait_send()
        last_copy(1, n).wait_send()
        return 0

    lax.fori_loop(1, 16, last_done, 0)


def on_device(perambulator, elementals, momentum, routes, node_of, owner_slot):
    vmem = pl.BlockSpec(memory_space=pltpu.VMEM)
    smem = pl.BlockSpec(memory_space=pltpu.SMEM)
    dma = pltpu.SemaphoreType.DMA
    out = pl.pallas_call(
        kernel,
        out_shape=jax.ShapeDtypeStruct((2, 8, 1024), F32),
        in_specs=[smem, smem, vmem, vmem, vmem, pl.BlockSpec(memory_space=pl.ANY)],
        out_specs=vmem,
        scratch_shapes=[
            pltpu.VMEM((2, 1024, 1024), BF16),
            pltpu.VMEM((8, 4, 256, 256), BF16),
            pltpu.VMEM((8, 2, 32, 256), BF16),
            pltpu.VMEM((512, 256), BF16),
            pltpu.VMEM((256, 256), BF16),
            pltpu.VMEM((256, 256), BF16),
            pltpu.VMEM((1024, 1024), BF16),
            pltpu.VMEM((4, 16, 256, 128), BF16),
            pltpu.VMEM((4, 16, 256, 128), BF16),
            pltpu.VMEM((4, 512, 2048), BF16),
            pltpu.VMEM((16, 256, 256), F32),
            pltpu.VMEM((16, 256, 256), BF16),
            pltpu.VMEM((16, 256, 256), BF16),
            pltpu.VMEM((3, 4, 256, 256), BF16),
            pltpu.VMEM((3, 4, 256, 256), BF16),
            pltpu.VMEM((4, 256, 256), F32),
            pltpu.VMEM((2, 16, 16, 512), BF16),
            pltpu.VMEM((2, 16, 16, 512), BF16),
            dma, dma((8,)), dma((8,)), dma((4, 16)), dma((4, 16)),
            dma((16,)), dma((16,)), dma((3, 4)), dma((3, 4)),
            dma((2, 16)), dma((2, 16)),
        ],
        compiler_params=pltpu.CompilerParams(
            collective_id=0, has_side_effects=True, vmem_limit_bytes=60 * 2**20
        ),
        cost_estimate=pl.CostEstimate(flops=20 * 10**9, bytes_accessed=8 * 2**20, transcendentals=0),
    )(
        momentum,
        owner_slot,
        elementals[0],
        routes[0, :, :, 0],
        node_of[0],
        perambulator[0, 0],
    )
    return out[None]


def solution(mesh):
    placed = (
        P("src", "snk", None, None, None),
        P("snk", None, None, "src", None),
        P("snk"),
        P("src", None, None, None),
        P("src", None, None),
        P(),
    )
    return jax.shard_map(
        on_device,
        mesh=mesh,
        in_specs=placed,
        out_specs=P("snk", None, "src", None),
        check_vma=False,
    )
```

```python
import jax
import jax.numpy as jnp
from jax import lax
from jax.experimental import pallas as pl
from jax.experimental.pallas import tpu as pltpu
from jax.sharding import PartitionSpec as P

MESH = pl.DeviceIdType.MESH
F32 = jnp.float32
BF16 = jnp.bfloat16
PIECES = 4
AHEAD = 9
SORTED_FIRST = 4


def packed(values, bits):
    return sum(value << (bits * n) for n, value in enumerate(values))


CHIPS = ((0, 1), (1, 1), (1, 0), (2, 1), (3, 1), (2, 0), (3, 0))
CHIPS_Y = packed([c[0] for c in CHIPS], 2)
CHIPS_Z = packed([c[1] for c in CHIPS], 1)
PEERS = (
    (0, 1, 0), (1, 1, 0), (1, 0, 0), (2, 1, 0), (3, 1, 0), (2, 0, 0), (0, 1, 1), (1, 1, 1),
    (3, 0, 0), (2, 1, 1), (3, 1, 1), (1, 0, 1), (2, 0, 1), (3, 0, 1), (0, 0, 1),
)
PEERS_Y = packed([p[0] for p in PEERS], 2)
PEERS_Z = packed([p[1] for p in PEERS], 1)
PEERS_C = packed([p[2] for p in PEERS], 1)
SHARES = packed((1, 2, 3, 0), 2)

def iota(shape, dim):
    return lax.broadcasted_iota(jnp.int32, shape, dim)


def dot(a, b):
    return jnp.dot(a, b, preferred_element_type=F32)


def dot_nt(a, b):
    return lax.dot_general(a, b, (((1,), (1,)), ((), ())), preferred_element_type=F32)


def kernel(
    momentum, owner_slot, elementals, routes, node_of, tile_hbm, out_ref,
    tile, right, phi, placed, select, rows_order, lane_order,
    sent, held, factor, kept, core_out, core_in,
    x_out, x_in, own_sum, last_out, last_in,
    tile_sem, phi_s, phi_r, ex_s, ex_r, core_s, core_r, x_s, x_r, last_s, last_r,
):
    source = lax.axis_index("src")
    sink = lax.axis_index("snk")
    zl, xx = source >> 2, source & 3
    yy, zh, core = sink >> 2, (sink >> 1) & 1, sink & 1

    load = pltpu.make_async_copy(tile_hbm, tile, tile_sem)
    load.start()

    barrier = pltpu.get_barrier_semaphore()

    def greet(there):
        pl.semaphore_signal(barrier, inc=1, device_id=there, device_id_type=MESH)

    def greet_source(n, _):
        greet(((source + n) & 7, sink))
        return 0

    def greet_sink(n, _):
        greet((source, (sink + n) & 15))
        return 0

    def greet_other(n, _):
        greet((source ^ 4, (sink + 2 * n) & 15))
        return 0

    lax.fori_loop(1, 8, greet_source, 0)
    lax.fori_loop(1, 16, greet_sink, 0)
    lax.fori_loop(1, 8, greet_other, 0)

    row, col = iota((256, 256), 0), iota((256, 256), 1)
    chosen = elementals[momentum[0]].reshape(64, 256)
    r64, c64 = iota((64, 64), 0), iota((64, 64), 1)
    wanted = ((r64 >> 3) & 1) * 32 + ((r64 >> 1) & 3) * 8 + (r64 >> 4) * 2 + (r64 & 1)
    pieces = jnp.where(c64 == wanted, 1.0, 0.0).astype(BF16)
    phi[source] = dot(pieces, chosen).astype(BF16).reshape(4, 16, 256)

    def chip_at(h):
        dy, dz = (CHIPS_Y >> (2 * h)) & 3, (CHIPS_Z >> h) & 1
        return ((yy + dy) & 3) * 2 + (zh ^ dz)

    def share(n):
        return (xx + (SHARES >> (2 * n))) & 3

    def peer_at(j):
        dy, dz, dc = (PEERS_Y >> (2 * j)) & 3, (PEERS_Z >> j) & 1, (PEERS_C >> j) & 1
        return ((yy + dy) & 3) * 4 + (zh ^ dz) * 2 + (core ^ dc)

    spins = jnp.where(col == (row & 63) * 4 + (row >> 6), 1.0, 0.0).astype(BF16)

    def by_spin(h, _):
        chip = chip_at(h)
        lanes = pl.ds(pl.multiple_of(chip * 128, 128), 128)
        for part in range(4):
            rows = slice(part * 256, (part + 1) * 256)
            both = jnp.concatenate([tile[0, rows, lanes], tile[1, rows, lanes]], axis=1)
            sorted_rows = dot(spins, both).astype(BF16)
            for a in range(4):
                right[chip, a, part * 64:(part + 1) * 64] = sorted_rows[a * 64:(a + 1) * 64]
        return 0


    pl.semaphore_wait(barrier, 29)

    def phi_copy(n, step):
        there = (source + step) & 7
        return pltpu.make_async_remote_copy(
            src_ref=phi.at[source, (there + (SHARES >> (2 * n))) & 3],
            dst_ref=phi.at[source, (there + (SHARES >> (2 * n))) & 3],
            send_sem=phi_s.at[n, step], recv_sem=phi_r.at[n, step],
            device_id=(there, sink), device_id_type=MESH,
        )

    def phi_arrival(n, step):
        owner = (source + 8 - step) & 7
        return pltpu.make_async_remote_copy(
            src_ref=phi.at[owner, share(n)], dst_ref=phi.at[owner, share(n)],
            send_sem=phi_s.at[n, step], recv_sem=phi_r.at[n, step],
            device_id=(owner, sink), device_id_type=MESH,
        )

    def phi_start(n):
        def one(step, _):
            phi_copy(n, step).start()
            return 0

        lax.fori_loop(1, 8, one, 0)

    phi_start(0)
    load.wait()
    lax.fori_loop(0, SORTED_FIRST, by_spin, 0)

    r128, c128 = iota((128, 128), 0), iota((128, 128), 1)
    wanted = ((r128 >> 1) & 7) * 16 + (r128 >> 6) * 8 + (r128 & 1) * 4 + ((r128 >> 5) & 1) * 2 + ((r128 >> 4) & 1)
    place = jnp.where(c128 == wanted, 1.0, 0.0).astype(BF16)

    def phi_place(n):
        def wait(step, _):
            phi_arrival(n, step).wait_recv()
            return 0

        lax.fori_loop(1, 8, wait, 0)
        whole = jnp.concatenate([phi[q, share(n)] for q in range(8)], axis=0)
        placed[n] = dot(place, whole).astype(BF16)

    for n in range(1, PIECES):
        phi_start(n)
    phi_place(0)
    low_lanes = iota((256, 128), 1) < 64

    def ex_copy(n, dest, origin):
        return pltpu.make_async_remote_copy(
            src_ref=sent.at[n, dest], dst_ref=held.at[n, origin],
            send_sem=ex_s.at[n, dest], recv_sem=ex_r.at[n, origin],
            device_id=(source, dest), device_id_type=MESH,
        )

    def columns(chip, a, start, stop):
        count = stop - start
        both = dot(placed[start:stop].reshape(count * 128, 256), right[chip, a])
        both = both.reshape(count, 2, 64, 256)
        real = (both[:, 0, :, :128] - both[:, 1, :, 128:]).reshape(count * 64, 128)
        imag = (both[:, 0, :, 128:] + both[:, 1, :, :128]).reshape(count * 64, 128)
        left = iota((count * 64, 128), 1) < 64
        low = jnp.where(left, real, pltpu.roll(imag, 64, 1)).astype(BF16)
        high = jnp.where(left, pltpu.roll(real, 64, 1), imag).astype(BF16)
        return low, high

    def dress_remote(h, start, stop):
        chip = chip_at(h)
        for a in range(4):
            low, high = columns(chip, a, start, stop)
            for n in range(start, stop):
                rows = slice((n - start) * 64, (n - start + 1) * 64)
                sent[n, 2 * chip, a * 64:(a + 1) * 64] = low[rows]
                sent[n, 2 * chip + 1, a * 64:(a + 1) * 64] = high[rows]

    partner = sink + 1 - 2 * core

    def dress_own(start, stop):
        for a in range(4):
            low, high = columns(yy * 2 + zh, a, start, stop)
            mine = jnp.where(core == 0, low, high)
            theirs = jnp.where(core == 0, high, low)
            for n in range(start, stop):
                rows = slice((n - start) * 64, (n - start + 1) * 64)
                held[n, sink, a * 64:(a + 1) * 64] = mine[rows]
                sent[n, partner, a * 64:(a + 1) * 64] = theirs[rows]

    def dress_first(h, _):
        chip = chip_at(h)
        dress_remote(h, 0, 1)
        ex_copy(0, 2 * chip, sink).start()
        ex_copy(0, 2 * chip + 1, sink).start()

        @pl.when(h + SORTED_FIRST < 8)
        def _():
            by_spin(h + SORTED_FIRST, 0)

        return 0

    lax.fori_loop(0, 7, dress_first, 0)
    dress_own(0, 1)
    ex_copy(0, partner, sink).start()
    for n in range(1, PIECES):
        phi_place(n)

    def dress_rest(h, _):
        dress_remote(h, 1, PIECES)
        return 0

    lax.fori_loop(0, 7, dress_rest, 0)
    dress_own(1, PIECES)

    def ex_send(n, j):
        return ex_copy(n, peer_at(j), sink)

    def ex_start(j, _):
        ex_send(1, j).start()
        return 0

    lax.fori_loop(0, AHEAD, ex_start, 0)

    position = jnp.zeros((16, 16), jnp.int32)
    for node in range(16):
        position = position + jnp.where(node_of[...] == node, owner_slot[node], 0)
    code = routes[...] * 16 + (position & 1) * 8 + (position >> 1)
    slab_row, slab_lane = iota((16, 256), 0), iota((16, 256), 1)
    widen = jnp.where((slab_lane & 15) == slab_row, 1.0, 0.0).astype(BF16)
    wide = dot(code.astype(F32).astype(BF16), widen)
    wide = jnp.where((slab_lane >> 4) == slab_row, wide, 0.0)
    named = jnp.sum(wide, axis=0, keepdims=True).astype(jnp.int32)
    select[...] = jnp.where(row == named, 1.0, 0.0).astype(BF16)

    spin, z_low, half, part, y_zh = row & 3, (row >> 4) & 1, (row >> 2) & 1, (row >> 3) & 1, row >> 5
    came = (spin << 6) | (z_low << 5) | (half << 4) | (part << 3) | y_zh
    rows_order[...] = jnp.where(col == came, 1.0, 0.0).astype(BF16)
    r, lane = iota((256, 1024), 0), iota((256, 1024), 1)
    target = (r & 15) * 64 + ((r >> 5) & 1) * 32 + ((r >> 4) & 1) * 4 + (r >> 6)
    for m in range(4):
        t = share(3 - m)
        lane_order[m * 256:(m + 1) * 256] = jnp.where(lane == target + t * 8, 1.0, 0.0).astype(BF16)

    def core_copy(g):
        return pltpu.make_async_remote_copy(
            src_ref=core_out.at[g], dst_ref=core_in.at[g],
            send_sem=core_s.at[g], recv_sem=core_r.at[g],
            device_id=(source, partner), device_id_type=MESH,
        )

    def x_copy(ni, tj):
        return pltpu.make_async_remote_copy(
            src_ref=x_out.at[ni, tj], dst_ref=x_in.at[ni, tj],
            send_sem=x_s.at[ni, tj], recv_sem=x_r.at[ni, tj],
            device_id=(zl * 4 + share(ni), sink), device_id_type=MESH,
        )

    def settle(g, ni, nj):
        core_copy(g).wait_recv()
        total = kept[g] + core_in[g].astype(F32)
        tj = share(nj)

        @pl.when(ni < 3)
        def _():
            x_out[ni, tj] = total.astype(BF16)
            x_copy(ni, tj).start()

        @pl.when(ni == 3)
        def _():
            own_sum[tj] = total

    def block(number, ni, nj, beside=()):
        side = jnp.concatenate([held[nj, r] for r in range(16)], axis=1)
        product = dot_nt(factor[ni], side)
        for pairing in beside:
            collect(nj, pairing)
        kept[number] = product[:256]
        core_out[number] = product[256:].astype(BF16)
        core_copy(number).start()

    def arrive(n):
        def one(j, _):
            ex_copy(n, sink, (sink + j + 1) & 15).wait_recv()
            over = jnp.where(j + AHEAD < 15, 0, 1)
            later, peer = n + 1 + over, j + AHEAD - 15 * over

            @pl.when(later < PIECES)
            def _():
                ex_send(n, j).wait_send()
                ex_send(later, peer).start()

            return 0

        lax.fori_loop(0, 15, one, 0)

    def earlier_blocks(n, base):
        def earlier(m, _):
            block(base + m, m, n)

            @pl.when(m > 0)
            def _():
                settle(base + m - 1, m - 1, n)

            return 0

        lax.fori_loop(0, n, earlier, 0)

    def collect(n, pairing):
        first = pl.ds(pl.multiple_of(pairing * 32, 32), 16)
        second = pl.ds(pl.multiple_of(pairing * 32 + 16, 16), 16)
        pair = [held[n, :, first, :].reshape(256, 128), held[n, :, second, :].reshape(256, 128)]
        sums = dot(select[...], jnp.concatenate(pair, axis=1))
        for k in range(2):
            plain = sums[:, k * 128:(k + 1) * 128]
            turned = pltpu.roll(plain, 64, 1)
            turned = jnp.where(low_lanes, turned, -turned)
            both = jnp.stack([plain.reshape(32, 8, 128), turned.reshape(32, 8, 128)], axis=1).astype(BF16)
            for r in range(16):
                for c in range(2):
                    rows = pl.ds(pl.multiple_of((core ^ c) * 256 + pairing * 32 + k * 16, 16), 16)
                    factor[n, rows, r * 128:(r + 1) * 128] = both[2 * r + c].reshape(16, 128)

    def collect_piece(n):
        def one(pairing, _):
            collect(n, pairing)
            return 0

        lax.fori_loop(0, 8, one, 0)

    def later_blocks(n, base, start, stop):
        def later(m, _):
            block(base + m, n, n - m)

            @pl.when(m > 0)
            def _():
                settle(base + m - 1, n, n - m + 1)

            return 0

        lax.fori_loop(start, stop, later, 0)

    def last_copy(side, n):
        there = (mine + n) & 15
        return pltpu.make_async_remote_copy(
            src_ref=last_out.at[side, there], dst_ref=last_in.at[side, n],
            send_sem=last_s.at[side, n], recv_sem=last_r.at[side, n],
            device_id=((there & 1) * 4 + xx, (there >> 1) * 2 + core), device_id_type=MESH,
        )

    def sum_x(side):
        for k in range(2):
            tj = share(3 - 2 * side - k)
            summed = own_sum[tj]
            for ni in range(3):
                x_copy(ni, tj).wait_recv()
                summed = summed + x_in[ni, tj].astype(F32)
            ordered = dot(rows_order[...], summed.astype(BF16)).astype(BF16)
            last_out[side, :, :, k * 256:(k + 1) * 256] = ordered.reshape(16, 16, 256)

        def last_start(n, _):
            last_copy(side, n).start()
            return 0

        lax.fori_loop(1, 16, last_start, 0)

    def sum_yz(side):
        def last_sum(n, total):
            last_copy(side, n).wait_recv()
            return total + last_in[side, n].astype(F32)

        total = lax.fori_loop(1, 16, last_sum, last_out[side, mine].astype(F32))
        high = total.astype(BF16)
        rest = total - high.astype(F32)
        middle = rest.astype(BF16)
        low = (rest - middle.astype(F32)).astype(BF16)
        parts = dot(jnp.concatenate([high, middle, low], axis=0), lane_order[side * 512:(side + 1) * 512])
        return (parts[:16] + parts[16:32]) + parts[32:]

    mine = yy * 4 + zh * 2 + zl

    def piece(n, _):
        arrive(n)
        collect_piece(n)
        later_blocks(n, n * n, 0, n + 1)
        earlier_blocks(n, n * n + n + 1)
        settle(n * n + n, n, 0)

        @pl.when(n > 0)
        def _():
            settle(n * n + 2 * n, n - 1, n)

        return 0

    lax.fori_loop(0, 3, piece, 0)
    arrive(3)
    block(9, 0, 3, (0, 1, 2))
    block(10, 1, 3, (3, 4, 5))
    settle(9, 0, 3)
    block(11, 2, 3, (6, 7))
    settle(10, 1, 3)
    block(12, 3, 3)
    settle(11, 2, 3)
    later_blocks(3, 12, 1, 3)
    sum_x(0)
    later_blocks(3, 12, 3, 4)
    settle(15, 3, 0)
    sum_x(1)
    final = sum_yz(0) + sum_yz(1)
    out_ref[...] = final.reshape(2, 8, 1024)

    def phi_done(n, _):
        for step in range(1, 8):
            phi_copy(n, step).wait_send()
        return 0

    lax.fori_loop(0, PIECES, phi_done, 0)

    def ex_done(j, _):
        ex_send(3, j).wait_send()

        @pl.when(j >= 15 - AHEAD)
        def _():
            ex_send(2, j).wait_send()

        return 0

    lax.fori_loop(0, 15, ex_done, 0)

    def core_done(g, _):
        core_copy(g).wait_send()
        return 0

    lax.fori_loop(0, 16, core_done, 0)

    def x_done(g, _):
        x_copy(g // 4, g % 4).wait_send()
        return 0

    lax.fori_loop(0, 12, x_done, 0)

    def last_done(n, _):
        last_copy(0, n).wait_send()
        last_copy(1, n).wait_send()
        return 0

    lax.fori_loop(1, 16, last_done, 0)


def on_device(perambulator, elementals, momentum, routes, node_of, owner_slot):
    vmem = pl.BlockSpec(memory_space=pltpu.VMEM)
    smem = pl.BlockSpec(memory_space=pltpu.SMEM)
    dma = pltpu.SemaphoreType.DMA
    out = pl.pallas_call(
        kernel,
        out_shape=jax.ShapeDtypeStruct((2, 8, 1024), F32),
        in_specs=[smem, smem, vmem, vmem, vmem, pl.BlockSpec(memory_space=pl.ANY)],
        out_specs=vmem,
        scratch_shapes=[
            pltpu.VMEM((2, 1024, 1024), BF16),
            pltpu.VMEM((8, 4, 256, 256), BF16),
            pltpu.VMEM((8, 4, 16, 256), BF16),
            pltpu.VMEM((4, 128, 256), BF16),
            pltpu.VMEM((256, 256), BF16),
            pltpu.VMEM((256, 256), BF16),
            pltpu.VMEM((1024, 1024), BF16),
            pltpu.VMEM((4, 16, 256, 128), BF16),
            pltpu.VMEM((4, 16, 256, 128), BF16),
            pltpu.VMEM((4, 512, 2048), BF16),
            pltpu.VMEM((16, 256, 256), F32),
            pltpu.VMEM((16, 256, 256), BF16),
            pltpu.VMEM((16, 256, 256), BF16),
            pltpu.VMEM((3, 4, 256, 256), BF16),
            pltpu.VMEM((3, 4, 256, 256), BF16),
            pltpu.VMEM((4, 256, 256), F32),
            pltpu.VMEM((2, 16, 16, 512), BF16),
            pltpu.VMEM((2, 16, 16, 512), BF16),
            dma, dma((4, 8)), dma((4, 8)), dma((4, 16)), dma((4, 16)),
            dma((16,)), dma((16,)), dma((3, 4)), dma((3, 4)),
            dma((2, 16)), dma((2, 16)),
        ],
        compiler_params=pltpu.CompilerParams(
            collective_id=0, has_side_effects=True, vmem_limit_bytes=60 * 2**20
        ),
        cost_estimate=pl.CostEstimate(flops=20 * 10**9, bytes_accessed=8 * 2**20, transcendentals=0),
    )(
        momentum,
        owner_slot,
        elementals[0],
        routes[0, :, :, 0],
        node_of[0],
        perambulator[0, 0],
    )
    return out[None]


def solution(mesh):
    placed = (
        P("src", "snk", None, None, None),
        P("snk", None, None, "src", None),
        P("snk"),
        P("src", None, None, None),
        P("src", None, None),
        P(),
    )
    return jax.shard_map(
        on_device,
        mesh=mesh,
        in_specs=placed,
        out_specs=P("snk", None, "src", None),
        check_vma=False,
    )
```

```python
import jax
import jax.numpy as jnp
from jax import lax
from jax.experimental import pallas as pl
from jax.experimental.pallas import tpu as pltpu
from jax.sharding import PartitionSpec as P

MESH = pl.DeviceIdType.MESH
F32 = jnp.float32
BF16 = jnp.bfloat16
PIECES = 4
AHEAD = 9
SORTED_FIRST = 4


def packed(values, bits):
    return sum(value << (bits * n) for n, value in enumerate(values))


CHIPS = ((0, 1), (1, 1), (1, 0), (2, 1), (3, 1), (2, 0), (3, 0))
CHIPS_Y = packed([c[0] for c in CHIPS], 2)
CHIPS_Z = packed([c[1] for c in CHIPS], 1)
PEERS = (
    (0, 1, 0), (1, 1, 0), (1, 0, 0), (2, 1, 0), (3, 1, 0), (2, 0, 0), (0, 1, 1), (1, 1, 1),
    (3, 0, 0), (2, 1, 1), (3, 1, 1), (1, 0, 1), (2, 0, 1), (3, 0, 1), (0, 0, 1),
)
PEERS_Y = packed([p[0] for p in PEERS], 2)
PEERS_Z = packed([p[1] for p in PEERS], 1)
PEERS_C = packed([p[2] for p in PEERS], 1)
SHARES = packed((1, 2, 3, 0), 2)

def iota(shape, dim):
    return lax.broadcasted_iota(jnp.int32, shape, dim)


def dot(a, b):
    return jnp.dot(a, b, preferred_element_type=F32)


def dot_nt(a, b):
    return lax.dot_general(a, b, (((1,), (1,)), ((), ())), preferred_element_type=F32)


def kernel(
    momentum_in, owner_slot_in, elementals_in, routes_in, node_of_in, tile_in, out_ref,
    momentum, owner_slot, elementals, routes, node_of,
    tile, right, phi, placed, select, rows_order, lane_order,
    sent, held, factor, kept, core_out, core_in,
    x_out, x_in, own_sum, last_out, last_in,
    load_sem, phi_s, phi_r, ex_s, ex_r, core_s, core_r, x_s, x_r, last_s, last_r,
):
    source = lax.axis_index("src")
    sink = lax.axis_index("snk")
    zl, xx = source >> 2, source & 3
    yy, zh, core = sink >> 2, (sink >> 1) & 1, sink & 1

    barrier = pltpu.get_barrier_semaphore()

    def greet(there):
        pl.semaphore_signal(barrier, inc=1, device_id=there, device_id_type=MESH)

    def greet_source(n, _):
        greet(((source + n) & 7, sink))
        return 0

    def greet_sink(n, _):
        greet((source, (sink + n) & 15))
        return 0

    def greet_other(n, _):
        greet((source ^ 4, (sink + 2 * n) & 15))
        return 0

    lax.fori_loop(1, 8, greet_source, 0)
    lax.fori_loop(1, 16, greet_sink, 0)
    lax.fori_loop(1, 8, greet_other, 0)

    loads = [
        pltpu.make_async_copy(momentum_in, momentum, load_sem.at[0]),
        pltpu.make_async_copy(elementals_in, elementals, load_sem.at[1]),
        pltpu.make_async_copy(tile_in, tile, load_sem.at[2]),
        pltpu.make_async_copy(routes_in, routes, load_sem.at[3]),
        pltpu.make_async_copy(node_of_in, node_of, load_sem.at[4]),
        pltpu.make_async_copy(owner_slot_in, owner_slot, load_sem.at[5]),
    ]
    for load in loads:
        load.start()

    row, col = iota((256, 256), 0), iota((256, 256), 1)
    loads[0].wait()
    loads[1].wait()
    chosen = elementals[momentum[0]].reshape(64, 256)
    r64, c64 = iota((64, 64), 0), iota((64, 64), 1)
    wanted = ((r64 >> 3) & 1) * 32 + ((r64 >> 1) & 3) * 8 + (r64 >> 4) * 2 + (r64 & 1)
    pieces = jnp.where(c64 == wanted, 1.0, 0.0).astype(BF16)
    phi[source] = dot(pieces, chosen).astype(BF16).reshape(4, 16, 256)

    def chip_at(h):
        dy, dz = (CHIPS_Y >> (2 * h)) & 3, (CHIPS_Z >> h) & 1
        return ((yy + dy) & 3) * 2 + (zh ^ dz)

    def share(n):
        return (xx + (SHARES >> (2 * n))) & 3

    def peer_at(j):
        dy, dz, dc = (PEERS_Y >> (2 * j)) & 3, (PEERS_Z >> j) & 1, (PEERS_C >> j) & 1
        return ((yy + dy) & 3) * 4 + (zh ^ dz) * 2 + (core ^ dc)

    spins = jnp.where(col == (row & 63) * 4 + (row >> 6), 1.0, 0.0).astype(BF16)

    def by_spin(h, _):
        chip = chip_at(h)
        lanes = pl.ds(pl.multiple_of(chip * 128, 128), 128)
        for part in range(4):
            rows = slice(part * 256, (part + 1) * 256)
            both = jnp.concatenate([tile[0, rows, lanes], tile[1, rows, lanes]], axis=1)
            sorted_rows = dot(spins, both).astype(BF16)
            for a in range(4):
                right[chip, a, part * 64:(part + 1) * 64] = sorted_rows[a * 64:(a + 1) * 64]
        return 0


    pl.semaphore_wait(barrier, 29)

    def phi_copy(n, step):
        there = (source + step) & 7
        return pltpu.make_async_remote_copy(
            src_ref=phi.at[source, (there + (SHARES >> (2 * n))) & 3],
            dst_ref=phi.at[source, (there + (SHARES >> (2 * n))) & 3],
            send_sem=phi_s.at[n, step], recv_sem=phi_r.at[n, step],
            device_id=(there, sink), device_id_type=MESH,
        )

    def phi_arrival(n, step):
        owner = (source + 8 - step) & 7
        return pltpu.make_async_remote_copy(
            src_ref=phi.at[owner, share(n)], dst_ref=phi.at[owner, share(n)],
            send_sem=phi_s.at[n, step], recv_sem=phi_r.at[n, step],
            device_id=(owner, sink), device_id_type=MESH,
        )

    def phi_start(n):
        def one(step, _):
            phi_copy(n, step).start()
            return 0

        lax.fori_loop(1, 8, one, 0)

    phi_start(0)
    loads[2].wait()
    lax.fori_loop(0, SORTED_FIRST, by_spin, 0)

    r128, c128 = iota((128, 128), 0), iota((128, 128), 1)
    wanted = ((r128 >> 1) & 7) * 16 + (r128 >> 6) * 8 + (r128 & 1) * 4 + ((r128 >> 5) & 1) * 2 + ((r128 >> 4) & 1)
    place = jnp.where(c128 == wanted, 1.0, 0.0).astype(BF16)

    def phi_place(n):
        def wait(step, _):
            phi_arrival(n, step).wait_recv()
            return 0

        lax.fori_loop(1, 8, wait, 0)
        whole = jnp.concatenate([phi[q, share(n)] for q in range(8)], axis=0)
        placed[n] = dot(place, whole).astype(BF16)

    for n in range(1, PIECES):
        phi_start(n)
    phi_place(0)
    low_lanes = iota((256, 128), 1) < 64

    def ex_copy(n, dest, origin):
        return pltpu.make_async_remote_copy(
            src_ref=sent.at[n, dest], dst_ref=held.at[n, origin],
            send_sem=ex_s.at[n, dest], recv_sem=ex_r.at[n, origin],
            device_id=(source, dest), device_id_type=MESH,
        )

    def columns(chip, a, start, stop):
        count = stop - start
        both = dot(placed[start:stop].reshape(count * 128, 256), right[chip, a])
        both = both.reshape(count, 2, 64, 256)
        real = (both[:, 0, :, :128] - both[:, 1, :, 128:]).reshape(count * 64, 128)
        imag = (both[:, 0, :, 128:] + both[:, 1, :, :128]).reshape(count * 64, 128)
        left = iota((count * 64, 128), 1) < 64
        low = jnp.where(left, real, pltpu.roll(imag, 64, 1)).astype(BF16)
        high = jnp.where(left, pltpu.roll(real, 64, 1), imag).astype(BF16)
        return low, high

    def dress_remote(h, start, stop):
        chip = chip_at(h)
        for a in range(4):
            low, high = columns(chip, a, start, stop)
            for n in range(start, stop):
                rows = slice((n - start) * 64, (n - start + 1) * 64)
                sent[n, 2 * chip, a * 64:(a + 1) * 64] = low[rows]
                sent[n, 2 * chip + 1, a * 64:(a + 1) * 64] = high[rows]

    partner = sink + 1 - 2 * core

    def dress_own(start, stop):
        for a in range(4):
            low, high = columns(yy * 2 + zh, a, start, stop)
            mine = jnp.where(core == 0, low, high)
            theirs = jnp.where(core == 0, high, low)
            for n in range(start, stop):
                rows = slice((n - start) * 64, (n - start + 1) * 64)
                held[n, sink, a * 64:(a + 1) * 64] = mine[rows]
                sent[n, partner, a * 64:(a + 1) * 64] = theirs[rows]

    def dress_first(h, _):
        chip = chip_at(h)
        dress_remote(h, 0, 1)
        ex_copy(0, 2 * chip, sink).start()
        ex_copy(0, 2 * chip + 1, sink).start()

        @pl.when(h + SORTED_FIRST < 8)
        def _():
            by_spin(h + SORTED_FIRST, 0)

        return 0

    lax.fori_loop(0, 7, dress_first, 0)
    dress_own(0, 1)
    ex_copy(0, partner, sink).start()
    for n in range(1, PIECES):
        phi_place(n)

    def dress_rest(h, _):
        dress_remote(h, 1, PIECES)
        return 0

    lax.fori_loop(0, 7, dress_rest, 0)
    dress_own(1, PIECES)

    def ex_send(n, j):
        return ex_copy(n, peer_at(j), sink)

    def ex_start(j, _):
        ex_send(1, j).start()
        return 0

    lax.fori_loop(0, AHEAD, ex_start, 0)

    for load in loads[3:]:
        load.wait()
    position = jnp.zeros((16, 16), jnp.int32)
    for node in range(16):
        position = position + jnp.where(node_of[...] == node, owner_slot[node], 0)
    code = routes[...] * 16 + (position & 1) * 8 + (position >> 1)
    slab_row, slab_lane = iota((16, 256), 0), iota((16, 256), 1)
    widen = jnp.where((slab_lane & 15) == slab_row, 1.0, 0.0).astype(BF16)
    wide = dot(code.astype(F32).astype(BF16), widen)
    wide = jnp.where((slab_lane >> 4) == slab_row, wide, 0.0)
    named = jnp.sum(wide, axis=0, keepdims=True).astype(jnp.int32)
    select[...] = jnp.where(row == named, 1.0, 0.0).astype(BF16)

    spin, z_low, half, part, y_zh = row & 3, (row >> 4) & 1, (row >> 2) & 1, (row >> 3) & 1, row >> 5
    came = (spin << 6) | (z_low << 5) | (half << 4) | (part << 3) | y_zh
    rows_order[...] = jnp.where(col == came, 1.0, 0.0).astype(BF16)
    r, lane = iota((256, 1024), 0), iota((256, 1024), 1)
    target = (r & 15) * 64 + ((r >> 5) & 1) * 32 + ((r >> 4) & 1) * 4 + (r >> 6)
    for m in range(4):
        t = share(3 - m)
        lane_order[m * 256:(m + 1) * 256] = jnp.where(lane == target + t * 8, 1.0, 0.0).astype(BF16)

    def core_copy(g):
        return pltpu.make_async_remote_copy(
            src_ref=core_out.at[g], dst_ref=core_in.at[g],
            send_sem=core_s.at[g], recv_sem=core_r.at[g],
            device_id=(source, partner), device_id_type=MESH,
        )

    def x_copy(ni, tj):
        return pltpu.make_async_remote_copy(
            src_ref=x_out.at[ni, tj], dst_ref=x_in.at[ni, tj],
            send_sem=x_s.at[ni, tj], recv_sem=x_r.at[ni, tj],
            device_id=(zl * 4 + share(ni), sink), device_id_type=MESH,
        )

    def settle(g, ni, nj):
        core_copy(g).wait_recv()
        total = kept[g] + core_in[g].astype(F32)
        tj = share(nj)

        @pl.when(ni < 3)
        def _():
            x_out[ni, tj] = total.astype(BF16)
            x_copy(ni, tj).start()

        @pl.when(ni == 3)
        def _():
            own_sum[tj] = total

    def block(number, ni, nj, beside=()):
        side = jnp.concatenate([held[nj, r] for r in range(16)], axis=1)
        product = dot_nt(factor[ni], side)
        for pairing in beside:
            collect(nj, pairing)
        kept[number] = product[:256]
        core_out[number] = product[256:].astype(BF16)
        core_copy(number).start()

    def arrive(n):
        def one(j, _):
            ex_copy(n, sink, (sink + j + 1) & 15).wait_recv()
            over = jnp.where(j + AHEAD < 15, 0, 1)
            later, peer = n + 1 + over, j + AHEAD - 15 * over

            @pl.when(later < PIECES)
            def _():
                ex_send(n, j).wait_send()
                ex_send(later, peer).start()

            return 0

        lax.fori_loop(0, 15, one, 0)

    def earlier_blocks(n, base):
        def earlier(m, _):
            block(base + m, m, n)

            @pl.when(m > 0)
            def _():
                settle(base + m - 1, m - 1, n)

            return 0

        lax.fori_loop(0, n, earlier, 0)

    def collect(n, pairing):
        first = pl.ds(pl.multiple_of(pairing * 32, 32), 16)
        second = pl.ds(pl.multiple_of(pairing * 32 + 16, 16), 16)
        pair = [held[n, :, first, :].reshape(256, 128), held[n, :, second, :].reshape(256, 128)]
        sums = dot(select[...], jnp.concatenate(pair, axis=1))
        for k in range(2):
            plain = sums[:, k * 128:(k + 1) * 128]
            turned = pltpu.roll(plain, 64, 1)
            turned = jnp.where(low_lanes, turned, -turned)
            both = jnp.stack([plain.reshape(32, 8, 128), turned.reshape(32, 8, 128)], axis=1).astype(BF16)
            for r in range(16):
                for c in range(2):
                    rows = pl.ds(pl.multiple_of((core ^ c) * 256 + pairing * 32 + k * 16, 16), 16)
                    factor[n, rows, r * 128:(r + 1) * 128] = both[2 * r + c].reshape(16, 128)

    def collect_piece(n):
        def one(pairing, _):
            collect(n, pairing)
            return 0

        lax.fori_loop(0, 8, one, 0)

    def later_blocks(n, base, start, stop):
        def later(m, _):
            block(base + m, n, n - m)

            @pl.when(m > 0)
            def _():
                settle(base + m - 1, n, n - m + 1)

            return 0

        lax.fori_loop(start, stop, later, 0)

    def last_copy(side, n):
        there = (mine + n) & 15
        return pltpu.make_async_remote_copy(
            src_ref=last_out.at[side, there], dst_ref=last_in.at[side, n],
            send_sem=last_s.at[side, n], recv_sem=last_r.at[side, n],
            device_id=((there & 1) * 4 + xx, (there >> 1) * 2 + core), device_id_type=MESH,
        )

    def sum_x(side):
        for k in range(2):
            tj = share(3 - 2 * side - k)
            summed = own_sum[tj]
            for ni in range(3):
                x_copy(ni, tj).wait_recv()
                summed = summed + x_in[ni, tj].astype(F32)
            ordered = dot(rows_order[...], summed.astype(BF16)).astype(BF16)
            last_out[side, :, :, k * 256:(k + 1) * 256] = ordered.reshape(16, 16, 256)

        def last_start(n, _):
            last_copy(side, n).start()
            return 0

        lax.fori_loop(1, 16, last_start, 0)

    def sum_yz(side):
        def last_sum(n, total):
            last_copy(side, n).wait_recv()
            return total + last_in[side, n].astype(F32)

        total = lax.fori_loop(1, 16, last_sum, last_out[side, mine].astype(F32))
        high = total.astype(BF16)
        rest = total - high.astype(F32)
        middle = rest.astype(BF16)
        low = (rest - middle.astype(F32)).astype(BF16)
        parts = dot(jnp.concatenate([high, middle, low], axis=0), lane_order[side * 512:(side + 1) * 512])
        return (parts[:16] + parts[16:32]) + parts[32:]

    mine = yy * 4 + zh * 2 + zl

    def piece(n, _):
        arrive(n)
        collect_piece(n)
        later_blocks(n, n * n, 0, n + 1)
        earlier_blocks(n, n * n + n + 1)
        settle(n * n + n, n, 0)

        @pl.when(n > 0)
        def _():
            settle(n * n + 2 * n, n - 1, n)

        return 0

    lax.fori_loop(0, 3, piece, 0)
    arrive(3)
    block(9, 0, 3, (0, 1, 2))
    block(10, 1, 3, (3, 4, 5))
    settle(9, 0, 3)
    block(11, 2, 3, (6, 7))
    settle(10, 1, 3)
    block(12, 3, 3)
    settle(11, 2, 3)
    later_blocks(3, 12, 1, 3)
    sum_x(0)
    later_blocks(3, 12, 3, 4)
    settle(15, 3, 0)
    sum_x(1)
    final = sum_yz(0) + sum_yz(1)
    out_ref[...] = final.reshape(2, 8, 1024)

    def phi_done(n, _):
        for step in range(1, 8):
            phi_copy(n, step).wait_send()
        return 0

    lax.fori_loop(0, PIECES, phi_done, 0)

    def ex_done(j, _):
        ex_send(3, j).wait_send()

        @pl.when(j >= 15 - AHEAD)
        def _():
            ex_send(2, j).wait_send()

        return 0

    lax.fori_loop(0, 15, ex_done, 0)

    def core_done(g, _):
        core_copy(g).wait_send()
        return 0

    lax.fori_loop(0, 16, core_done, 0)

    def x_done(g, _):
        x_copy(g // 4, g % 4).wait_send()
        return 0

    lax.fori_loop(0, 12, x_done, 0)

    def last_done(n, _):
        last_copy(0, n).wait_send()
        last_copy(1, n).wait_send()
        return 0

    lax.fori_loop(1, 16, last_done, 0)


def on_device(perambulator, elementals, momentum, routes, node_of, owner_slot):
    vmem = pl.BlockSpec(memory_space=pltpu.VMEM)
    dma = pltpu.SemaphoreType.DMA
    out = pl.pallas_call(
        kernel,
        out_shape=jax.ShapeDtypeStruct((2, 8, 1024), F32),
        in_specs=[pl.BlockSpec(memory_space=pl.ANY)] * 6,
        out_specs=vmem,
        scratch_shapes=[
            pltpu.SMEM((1,), jnp.int32),
            pltpu.SMEM((16,), jnp.int32),
            pltpu.VMEM((4, 2, 32, 256), BF16),
            pltpu.VMEM((16, 16), jnp.int32),
            pltpu.VMEM((16, 16), jnp.int32),
            pltpu.VMEM((2, 1024, 1024), BF16),
            pltpu.VMEM((8, 4, 256, 256), BF16),
            pltpu.VMEM((8, 4, 16, 256), BF16),
            pltpu.VMEM((4, 128, 256), BF16),
            pltpu.VMEM((256, 256), BF16),
            pltpu.VMEM((256, 256), BF16),
            pltpu.VMEM((1024, 1024), BF16),
            pltpu.VMEM((4, 16, 256, 128), BF16),
            pltpu.VMEM((4, 16, 256, 128), BF16),
            pltpu.VMEM((4, 512, 2048), BF16),
            pltpu.VMEM((16, 256, 256), F32),
            pltpu.VMEM((16, 256, 256), BF16),
            pltpu.VMEM((16, 256, 256), BF16),
            pltpu.VMEM((3, 4, 256, 256), BF16),
            pltpu.VMEM((3, 4, 256, 256), BF16),
            pltpu.VMEM((4, 256, 256), F32),
            pltpu.VMEM((2, 16, 16, 512), BF16),
            pltpu.VMEM((2, 16, 16, 512), BF16),
            dma((6,)), dma((4, 8)), dma((4, 8)), dma((4, 16)), dma((4, 16)),
            dma((16,)), dma((16,)), dma((3, 4)), dma((3, 4)),
            dma((2, 16)), dma((2, 16)),
        ],
        compiler_params=pltpu.CompilerParams(
            collective_id=0, has_side_effects=True, vmem_limit_bytes=60 * 2**20
        ),
        cost_estimate=pl.CostEstimate(flops=20 * 10**9, bytes_accessed=8 * 2**20, transcendentals=0),
    )(
        momentum,
        owner_slot,
        elementals[0],
        routes[0, :, :, 0],
        node_of[0],
        perambulator[0, 0],
    )
    return out[None]


def solution(mesh):
    placed = (
        P("src", "snk", None, None, None),
        P("snk", None, None, "src", None),
        P("snk"),
        P("src", None, None, None),
        P("src", None, None),
        P(),
    )
    return jax.shard_map(
        on_device,
        mesh=mesh,
        in_specs=placed,
        out_specs=P("snk", None, "src", None),
        check_vma=False,
    )
```

```python
import jax
import jax.numpy as jnp
from jax import lax
from jax.experimental import pallas as pl
from jax.experimental.pallas import tpu as pltpu
from jax.sharding import PartitionSpec as P

MESH = pl.DeviceIdType.MESH
F32 = jnp.float32
BF16 = jnp.bfloat16
PIECES = 4
AHEAD = 9
SORTED_FIRST = 4


def packed(values, bits):
    return sum(value << (bits * n) for n, value in enumerate(values))


CHIPS = ((0, 1), (1, 1), (1, 0), (2, 1), (3, 1), (2, 0), (3, 0))
CHIPS_Y = packed([c[0] for c in CHIPS], 2)
CHIPS_Z = packed([c[1] for c in CHIPS], 1)
PEERS = (
    (0, 1, 0), (1, 1, 0), (1, 0, 0), (2, 1, 0), (3, 1, 0), (2, 0, 0), (0, 1, 1), (1, 1, 1),
    (3, 0, 0), (2, 1, 1), (3, 1, 1), (1, 0, 1), (2, 0, 1), (3, 0, 1), (0, 0, 1),
)
PEERS_Y = packed([p[0] for p in PEERS], 2)
PEERS_Z = packed([p[1] for p in PEERS], 1)
PEERS_C = packed([p[2] for p in PEERS], 1)
SHARES = packed((1, 2, 3, 0), 2)

def iota(shape, dim):
    return lax.broadcasted_iota(jnp.int32, shape, dim)


def dot(a, b):
    return jnp.dot(a, b, preferred_element_type=F32)


def dot_nt(a, b):
    return lax.dot_general(a, b, (((1,), (1,)), ((), ())), preferred_element_type=F32)


def kernel(
    momentum_in, owner_slot_in, elementals_in, routes_in, node_of_in, tile_in, out_ref,
    momentum, owner_slot, elementals, routes, node_of,
    tile, right, phi, placed, select, rows_order, lane_order,
    sent, held, factor, kept, core_out, core_in,
    x_out, x_in, own_sum, last_out, last_in,
    load_sem, phi_s, phi_r, ex_s, ex_r, core_s, core_r, x_s, x_r, last_s, last_r,
):
    source = lax.axis_index("src")
    sink = lax.axis_index("snk")
    zl, xx = source >> 2, source & 3
    yy, zh, core = sink >> 2, (sink >> 1) & 1, sink & 1

    barrier = pltpu.get_barrier_semaphore()

    def greet(there):
        pl.semaphore_signal(barrier, inc=1, device_id=there, device_id_type=MESH)

    def greet_source(n, _):
        greet(((source + n) & 7, sink))
        return 0

    def greet_sink(n, _):
        greet((source, (sink + n) & 15))
        return 0

    def greet_other(n, _):
        greet((source ^ 4, (sink + 2 * n) & 15))
        return 0

    lax.fori_loop(1, 8, greet_source, 0)
    lax.fori_loop(1, 16, greet_sink, 0)
    lax.fori_loop(1, 8, greet_other, 0)

    loads = [
        pltpu.make_async_copy(momentum_in, momentum, load_sem.at[0]),
        pltpu.make_async_copy(elementals_in, elementals, load_sem.at[1]),
        pltpu.make_async_copy(tile_in, tile, load_sem.at[2]),
        pltpu.make_async_copy(routes_in, routes, load_sem.at[3]),
        pltpu.make_async_copy(node_of_in, node_of, load_sem.at[4]),
        pltpu.make_async_copy(owner_slot_in, owner_slot, load_sem.at[5]),
    ]
    for load in loads:
        load.start()

    row, col = iota((256, 256), 0), iota((256, 256), 1)
    loads[0].wait()
    loads[1].wait()
    chosen = elementals[momentum[0]].reshape(64, 256)
    r64, c64 = iota((64, 64), 0), iota((64, 64), 1)
    wanted = ((r64 >> 3) & 1) * 32 + ((r64 >> 1) & 3) * 8 + (r64 >> 4) * 2 + (r64 & 1)
    pieces = jnp.where(c64 == wanted, 1.0, 0.0).astype(BF16)
    phi[source] = dot(pieces, chosen).astype(BF16).reshape(4, 16, 256)

    def chip_at(h):
        dy, dz = (CHIPS_Y >> (2 * h)) & 3, (CHIPS_Z >> h) & 1
        return ((yy + dy) & 3) * 2 + (zh ^ dz)

    def share(n):
        return (xx + (SHARES >> (2 * n))) & 3

    def peer_at(j):
        dy, dz, dc = (PEERS_Y >> (2 * j)) & 3, (PEERS_Z >> j) & 1, (PEERS_C >> j) & 1
        return ((yy + dy) & 3) * 4 + (zh ^ dz) * 2 + (core ^ dc)

    spins = jnp.where(col == (row & 63) * 4 + (row >> 6), 1.0, 0.0).astype(BF16)

    def by_spin(h, _):
        chip = chip_at(h)
        lanes = pl.ds(pl.multiple_of(chip * 128, 128), 128)
        for part in range(4):
            rows = slice(part * 256, (part + 1) * 256)
            both = jnp.concatenate([tile[0, rows, lanes], tile[1, rows, lanes]], axis=1)
            sorted_rows = dot(spins, both).astype(BF16)
            for a in range(4):
                right[chip, a, part * 64:(part + 1) * 64] = sorted_rows[a * 64:(a + 1) * 64]
        return 0


    pl.semaphore_wait(barrier, 29)

    def phi_copy(n, step):
        there = (source + step) & 7
        return pltpu.make_async_remote_copy(
            src_ref=phi.at[source, (there + (SHARES >> (2 * n))) & 3],
            dst_ref=phi.at[source, (there + (SHARES >> (2 * n))) & 3],
            send_sem=phi_s.at[n, step], recv_sem=phi_r.at[n, step],
            device_id=(there, sink), device_id_type=MESH,
        )

    def phi_arrival(n, step):
        owner = (source + 8 - step) & 7
        return pltpu.make_async_remote_copy(
            src_ref=phi.at[owner, share(n)], dst_ref=phi.at[owner, share(n)],
            send_sem=phi_s.at[n, step], recv_sem=phi_r.at[n, step],
            device_id=(owner, sink), device_id_type=MESH,
        )

    def phi_start(n):
        def one(step, _):
            phi_copy(n, step).start()
            return 0

        lax.fori_loop(1, 8, one, 0)

    phi_start(0)
    loads[2].wait()
    lax.fori_loop(0, SORTED_FIRST, by_spin, 0)

    r128, c128 = iota((128, 128), 0), iota((128, 128), 1)
    wanted = ((r128 >> 1) & 7) * 16 + (r128 >> 6) * 8 + (r128 & 1) * 4 + ((r128 >> 5) & 1) * 2 + ((r128 >> 4) & 1)
    place = jnp.where(c128 == wanted, 1.0, 0.0).astype(BF16)

    def phi_place(n):
        def wait(step, _):
            phi_arrival(n, step).wait_recv()
            return 0

        lax.fori_loop(1, 8, wait, 0)
        whole = jnp.concatenate([phi[q, share(n)] for q in range(8)], axis=0)
        placed[n] = dot(place, whole).astype(BF16)

    for n in range(1, PIECES):
        phi_start(n)
    phi_place(0)
    low_lanes = iota((256, 128), 1) < 64

    def ex_copy(n, dest, origin):
        return pltpu.make_async_remote_copy(
            src_ref=sent.at[n, dest], dst_ref=held.at[n, origin],
            send_sem=ex_s.at[n, dest], recv_sem=ex_r.at[n, origin],
            device_id=(source, dest), device_id_type=MESH,
        )

    def columns(chip, a, start, stop):
        count = stop - start
        both = dot(placed[start:stop].reshape(count * 128, 256), right[chip, a])
        both = both.reshape(count, 2, 64, 256)
        real = (both[:, 0, :, :128] - both[:, 1, :, 128:]).reshape(count * 64, 128)
        imag = (both[:, 0, :, 128:] + both[:, 1, :, :128]).reshape(count * 64, 128)
        left = iota((count * 64, 128), 1) < 64
        low = jnp.where(left, real, pltpu.roll(imag, 64, 1)).astype(BF16)
        high = jnp.where(left, pltpu.roll(real, 64, 1), imag).astype(BF16)
        return low, high

    def dress_remote(h, start, stop):
        chip = chip_at(h)
        for a in range(4):
            low, high = columns(chip, a, start, stop)
            for n in range(start, stop):
                rows = slice((n - start) * 64, (n - start + 1) * 64)
                sent[n, 2 * chip, a * 64:(a + 1) * 64] = low[rows]
                sent[n, 2 * chip + 1, a * 64:(a + 1) * 64] = high[rows]

    partner = sink + 1 - 2 * core

    def dress_own(start, stop):
        for a in range(4):
            low, high = columns(yy * 2 + zh, a, start, stop)
            mine = jnp.where(core == 0, low, high)
            theirs = jnp.where(core == 0, high, low)
            for n in range(start, stop):
                rows = slice((n - start) * 64, (n - start + 1) * 64)
                held[n, sink, a * 64:(a + 1) * 64] = mine[rows]
                sent[n, partner, a * 64:(a + 1) * 64] = theirs[rows]

    def dress_first(h, _):
        chip = chip_at(h)
        dress_remote(h, 0, 1)
        ex_copy(0, 2 * chip, sink).start()
        ex_copy(0, 2 * chip + 1, sink).start()

        @pl.when(h + SORTED_FIRST < 8)
        def _():
            by_spin(h + SORTED_FIRST, 0)

        return 0

    lax.fori_loop(0, 7, dress_first, 0)
    dress_own(0, 1)
    ex_copy(0, partner, sink).start()
    for n in range(1, PIECES):
        phi_place(n)

    def dress_rest(h, _):
        dress_remote(h, 1, PIECES)
        return 0

    lax.fori_loop(0, 7, dress_rest, 0)
    dress_own(1, PIECES)

    def ex_send(n, j):
        return ex_copy(n, peer_at(j), sink)

    def ex_start(j, _):
        ex_send(1, j).start()
        return 0

    lax.fori_loop(0, AHEAD, ex_start, 0)

    for load in loads[3:]:
        load.wait()
    position = jnp.zeros((16, 16), jnp.int32)
    for node in range(16):
        position = position + jnp.where(node_of[...] == node, owner_slot[node], 0)
    code = routes[...] * 16 + (position & 1) * 8 + (position >> 1)
    slab_row, slab_lane = iota((16, 256), 0), iota((16, 256), 1)
    widen = jnp.where((slab_lane & 15) == slab_row, 1.0, 0.0).astype(BF16)
    wide = dot(code.astype(F32).astype(BF16), widen)
    wide = jnp.where((slab_lane >> 4) == slab_row, wide, 0.0)
    named = jnp.sum(wide, axis=0, keepdims=True).astype(jnp.int32)
    select[...] = jnp.where(row == named, 1.0, 0.0).astype(BF16)

    spin, z_low, half, part, y_zh = row & 3, (row >> 4) & 1, (row >> 2) & 1, (row >> 3) & 1, row >> 5
    came = (spin << 6) | (z_low << 5) | (half << 4) | (part << 3) | y_zh
    rows_order[...] = jnp.where(col == came, 1.0, 0.0).astype(BF16)
    r, lane = iota((256, 1024), 0), iota((256, 1024), 1)
    target = (r & 15) * 64 + ((r >> 5) & 1) * 32 + ((r >> 4) & 1) * 4 + (r >> 6)
    for m in range(4):
        t = share(3 - m)
        lane_order[m * 256:(m + 1) * 256] = jnp.where(lane == target + t * 8, 1.0, 0.0).astype(BF16)

    def core_copy(g):
        return pltpu.make_async_remote_copy(
            src_ref=core_out.at[g], dst_ref=core_in.at[g],
            send_sem=core_s.at[g], recv_sem=core_r.at[g],
            device_id=(source, partner), device_id_type=MESH,
        )

    def x_copy(ni, tj):
        return pltpu.make_async_remote_copy(
            src_ref=x_out.at[ni, tj], dst_ref=x_in.at[ni, tj],
            send_sem=x_s.at[ni, tj], recv_sem=x_r.at[ni, tj],
            device_id=(zl * 4 + share(ni), sink), device_id_type=MESH,
        )

    def settle(g, ni, nj):
        core_copy(g).wait_recv()
        total = kept[g] + core_in[g].astype(F32)
        tj = share(nj)

        @pl.when(ni < 3)
        def _():
            x_out[ni, tj] = total.astype(BF16)
            x_copy(ni, tj).start()

        @pl.when(ni == 3)
        def _():
            own_sum[tj] = total

    def block(number, ni, nj, beside=()):
        side = jnp.concatenate([held[nj, r] for r in range(16)], axis=1)
        product = dot_nt(factor[ni], side)
        for pairing in beside:
            collect(nj, pairing)
        kept[number] = product[:256]
        core_out[number] = product[256:].astype(BF16)
        core_copy(number).start()

    def arrive(n):
        def one(j, _):
            ex_copy(n, sink, (sink + j + 1) & 15).wait_recv()
            over = jnp.where(j + AHEAD < 15, 0, 1)
            later, peer = n + 1 + over, j + AHEAD - 15 * over

            @pl.when(later < PIECES)
            def _():
                ex_send(n, j).wait_send()
                ex_send(later, peer).start()

            return 0

        lax.fori_loop(0, 15, one, 0)

    def earlier_blocks(n, base):
        def earlier(m, _):
            block(base + m, m, n)

            @pl.when(m > 0)
            def _():
                settle(base + m - 1, m - 1, n)

            return 0

        lax.fori_loop(0, n, earlier, 0)

    def collect(n, pairing):
        first = pl.ds(pl.multiple_of(pairing * 32, 32), 16)
        second = pl.ds(pl.multiple_of(pairing * 32 + 16, 16), 16)
        pair = [held[n, :, first, :].reshape(256, 128), held[n, :, second, :].reshape(256, 128)]
        sums = dot(select[...], jnp.concatenate(pair, axis=1))
        for k in range(2):
            plain = sums[:, k * 128:(k + 1) * 128]
            turned = pltpu.roll(plain, 64, 1)
            turned = jnp.where(low_lanes, turned, -turned)
            both = jnp.stack([plain.reshape(32, 8, 128), turned.reshape(32, 8, 128)], axis=1).astype(BF16)
            for r in range(16):
                for c in range(2):
                    rows = pl.ds(pl.multiple_of((core ^ c) * 256 + pairing * 32 + k * 16, 16), 16)
                    factor[n, rows, r * 128:(r + 1) * 128] = both[2 * r + c].reshape(16, 128)

    def collect_some(n, start, stop):
        def one(pairing, _):
            collect(n, pairing)
            return 0

        lax.fori_loop(start, stop, one, 0)

    def later_blocks(n, base, start, stop):
        def later(m, _):
            block(base + m, n, n - m)

            @pl.when(m > 0)
            def _():
                settle(base + m - 1, n, n - m + 1)

            return 0

        lax.fori_loop(start, stop, later, 0)

    def last_copy(side, n):
        there = (mine + n) & 15
        return pltpu.make_async_remote_copy(
            src_ref=last_out.at[side, there], dst_ref=last_in.at[side, n],
            send_sem=last_s.at[side, n], recv_sem=last_r.at[side, n],
            device_id=((there & 1) * 4 + xx, (there >> 1) * 2 + core), device_id_type=MESH,
        )

    def sum_x(side):
        for k in range(2):
            tj = share(3 - 2 * side - k)
            summed = own_sum[tj]
            for ni in range(3):
                x_copy(ni, tj).wait_recv()
                summed = summed + x_in[ni, tj].astype(F32)
            ordered = dot(rows_order[...], summed.astype(BF16)).astype(BF16)
            last_out[side, :, :, k * 256:(k + 1) * 256] = ordered.reshape(16, 16, 256)

        def last_start(n, _):
            last_copy(side, n).start()
            return 0

        lax.fori_loop(1, 16, last_start, 0)

    def sum_yz(side):
        def last_sum(n, total):
            last_copy(side, n).wait_recv()
            return total + last_in[side, n].astype(F32)

        total = lax.fori_loop(1, 16, last_sum, last_out[side, mine].astype(F32))
        high = total.astype(BF16)
        rest = total - high.astype(F32)
        middle = rest.astype(BF16)
        low = (rest - middle.astype(F32)).astype(BF16)
        parts = dot(jnp.concatenate([high, middle, low], axis=0), lane_order[side * 512:(side + 1) * 512])
        return (parts[:16] + parts[16:32]) + parts[32:]

    mine = yy * 4 + zh * 2 + zl

    def piece(n, _):
        arrive(n)
        collect_some(n, 0, 8)
        later_blocks(n, n * n, 0, n + 1)
        earlier_blocks(n, n * n + n + 1)
        settle(n * n + n, n, 0)

        @pl.when(n > 0)
        def _():
            settle(n * n + 2 * n, n - 1, n)

        return 0

    lax.fori_loop(0, 3, piece, 0)
    arrive(3)
    block(9, 0, 3)
    block(10, 1, 3)
    settle(9, 0, 3)
    block(11, 2, 3)
    settle(10, 1, 3)
    collect_some(3, 0, 3)
    settle(11, 2, 3)
    collect_some(3, 3, 8)
    block(12, 3, 3)
    later_blocks(3, 12, 1, 3)
    sum_x(0)
    later_blocks(3, 12, 3, 4)
    settle(15, 3, 0)
    sum_x(1)
    final = sum_yz(0) + sum_yz(1)
    out_ref[...] = final.reshape(2, 8, 1024)

    def phi_done(n, _):
        for step in range(1, 8):
            phi_copy(n, step).wait_send()
        return 0

    lax.fori_loop(0, PIECES, phi_done, 0)

    def ex_done(j, _):
        ex_send(3, j).wait_send()

        @pl.when(j >= 15 - AHEAD)
        def _():
            ex_send(2, j).wait_send()

        return 0

    lax.fori_loop(0, 15, ex_done, 0)

    def core_done(g, _):
        core_copy(g).wait_send()
        return 0

    lax.fori_loop(0, 16, core_done, 0)

    def x_done(g, _):
        x_copy(g // 4, g % 4).wait_send()
        return 0

    lax.fori_loop(0, 12, x_done, 0)

    def last_done(n, _):
        last_copy(0, n).wait_send()
        last_copy(1, n).wait_send()
        return 0

    lax.fori_loop(1, 16, last_done, 0)


def on_device(perambulator, elementals, momentum, routes, node_of, owner_slot):
    vmem = pl.BlockSpec(memory_space=pltpu.VMEM)
    dma = pltpu.SemaphoreType.DMA
    out = pl.pallas_call(
        kernel,
        out_shape=jax.ShapeDtypeStruct((2, 8, 1024), F32),
        in_specs=[pl.BlockSpec(memory_space=pl.ANY)] * 6,
        out_specs=vmem,
        scratch_shapes=[
            pltpu.SMEM((1,), jnp.int32),
            pltpu.SMEM((16,), jnp.int32),
            pltpu.VMEM((4, 2, 32, 256), BF16),
            pltpu.VMEM((16, 16), jnp.int32),
            pltpu.VMEM((16, 16), jnp.int32),
            pltpu.VMEM((2, 1024, 1024), BF16),
            pltpu.VMEM((8, 4, 256, 256), BF16),
            pltpu.VMEM((8, 4, 16, 256), BF16),
            pltpu.VMEM((4, 128, 256), BF16),
            pltpu.VMEM((256, 256), BF16),
            pltpu.VMEM((256, 256), BF16),
            pltpu.VMEM((1024, 1024), BF16),
            pltpu.VMEM((4, 16, 256, 128), BF16),
            pltpu.VMEM((4, 16, 256, 128), BF16),
            pltpu.VMEM((4, 512, 2048), BF16),
            pltpu.VMEM((16, 256, 256), F32),
            pltpu.VMEM((16, 256, 256), BF16),
            pltpu.VMEM((16, 256, 256), BF16),
            pltpu.VMEM((3, 4, 256, 256), BF16),
            pltpu.VMEM((3, 4, 256, 256), BF16),
            pltpu.VMEM((4, 256, 256), F32),
            pltpu.VMEM((2, 16, 16, 512), BF16),
            pltpu.VMEM((2, 16, 16, 512), BF16),
            dma((6,)), dma((4, 8)), dma((4, 8)), dma((4, 16)), dma((4, 16)),
            dma((16,)), dma((16,)), dma((3, 4)), dma((3, 4)),
            dma((2, 16)), dma((2, 16)),
        ],
        compiler_params=pltpu.CompilerParams(
            collective_id=0, has_side_effects=True, vmem_limit_bytes=60 * 2**20
        ),
        cost_estimate=pl.CostEstimate(flops=20 * 10**9, bytes_accessed=8 * 2**20, transcendentals=0),
    )(
        momentum,
        owner_slot,
        elementals[0],
        routes[0, :, :, 0],
        node_of[0],
        perambulator[0, 0],
    )
    return out[None]


def solution(mesh):
    placed = (
        P("src", "snk", None, None, None),
        P("snk", None, None, "src", None),
        P("snk"),
        P("src", None, None, None),
        P("src", None, None),
        P(),
    )
    return jax.shard_map(
        on_device,
        mesh=mesh,
        in_specs=placed,
        out_specs=P("snk", None, "src", None),
        check_vma=False,
    )
```
